128 devices in a mesh: group: 4 (over y), member: 32 (over z, x, core).
Axes of the slice: x: 4, y: 4, z: 4, core: 2. Of those that a mesh axis runs over, the one named last changes fastest.
Arguments:
- tokens: bfloat16 [256, 256, 1280], P(('group', 'member')), may hold values from -12 to 12
- slot_key_matrix: bfloat16 [1280, 128], replicated, may hold values from -2.5 to 2.5
- w_in: bfloat16 [128, 1280, 2560], P(('group', 'member')), may hold values from -0.15625 to 0.15625
- w_out: bfloat16 [128, 2560, 1280], P(('group', 'member')), may hold values from -0.125 to 0.125
- upstream: bfloat16 [256, 256, 1280], P(('group', 'member')), may hold values from -6 to 6
Outputs:
- mixed: bfloat16 [256, 256, 1280], P(('group', 'member'))
- token_grad: bfloat16 [256, 256, 1280], P(('group', 'member'))
- key_grad: float32 [128, 1280], P(('group', 'member'))
The draws below stay inside these ranges and needn't reach their ends.
All inputs are finite; a program needn't handle non-finite values.
Results may differ from the reference program's by a relative error of at most 0.014.
Values may be sent and summed in bfloat16 or wider, within the bound.
No kernel may reach another device: no remote copies, remote signals or barrier semaphores. Data moves between devices by JAX's collectives and lax.ppermute only.
A program may use at most 64 MiB of HBM per device.

```python
import math
import jax
import jax.numpy as jnp
from jax import lax

D = 1280
FF = 2560
PATCHES = 256
EXPERT_COUNT = 128
IMAGES = 256


def draw_slot_key_matrix(key, part):
    key = jax.random.fold_in(key, 11)
    spread = 3.0 / math.sqrt(D)
    base = jnp.clip(jax.random.normal(key, (D, EXPERT_COUNT), jnp.float32) * spread, -6.0 * spread, 6.0 * spread)
    return base.astype(jnp.bfloat16)


def draw_tokens(key, part):
    key = jax.random.fold_in(key, 23)
    base = jnp.clip(jax.random.normal(key, (IMAGES, PATCHES, D), jnp.float32), -6.0, 6.0)
    return base.astype(jnp.bfloat16)


def shard_levels(key, shape, pieces, least, largest):
    loudness, own = 1.0, jax.random.fold_in(key, 6)
    for axis_at, blocks in pieces:
        heights = jnp.exp(jax.random.uniform(jax.random.fold_in(own, axis_at), (blocks,), jnp.float32, least / len(pieces), largest / len(pieces)))
        loudness = loudness * jnp.repeat(heights, shape[axis_at] // blocks).reshape([-1 if axis == axis_at else 1 for axis in range(len(shape))])
    return loudness


def centred(own_key, dims, scale, most, cuts=(), kind=jnp.bfloat16):
    loudness = shard_levels(own_key, dims, cuts, -0.22, 0.18) if cuts else 1.0
    entries = jax.random.normal(own_key, dims, jnp.float32) * scale * loudness
    return jnp.minimum(jnp.maximum(entries, -most), most).astype(kind)


def setup_inputs(seed: int = 0) -> dict:
    keys = jax.random.split(jax.random.key(seed), 6)
    tokens = draw_tokens(jax.random.fold_in(keys[5], 71), 0)
    slot_key_matrix = draw_slot_key_matrix(jax.random.fold_in(keys[5], 71), 0)
    w_in = centred(keys[2], (EXPERT_COUNT, D, FF), D ** -0.5, 0.15625, ((0, 128),))
    w_out = centred(keys[3], (EXPERT_COUNT, FF, D), FF ** -0.5, 0.125, ((0, 128),))
    upstream = centred(keys[4], (IMAGES, PATCHES, D), 1.0, 6.0, ((0, 128),))
    return dict(tokens=tokens, slot_key_matrix=slot_key_matrix, w_in=w_in, w_out=w_out, upstream=upstream)


def gelu_tanh(value):
    return jax.nn.gelu(value, approximate=True)

def reference(tokens, slot_key_matrix, w_in, w_out, upstream):

    def weights(image):
        logits = jnp.dot(image, slot_key_matrix, preferred_element_type=jnp.float32)
        return (jax.nn.softmax(logits, axis=0), jax.nn.softmax(logits, axis=1))

    def dispatch_one(image):
        dispatch, unused = weights(image)
        return jnp.dot(dispatch.astype(jnp.bfloat16).T, image, preferred_element_type=jnp.float32).astype(jnp.bfloat16)
    slot_in = lax.map(dispatch_one, tokens)
    expert_rows = jnp.swapaxes(slot_in, 0, 1)

    def expert_forward(packed):
        slot_row_block, first_w, second_w = packed
        pre_act = jnp.dot(slot_row_block, first_w, preferred_element_type=jnp.float32)
        activated = gelu_tanh(pre_act).astype(jnp.bfloat16)
        return jnp.dot(activated, second_w, preferred_element_type=jnp.float32).astype(jnp.bfloat16)
    slot_out = jnp.swapaxes(lax.map(expert_forward, (expert_rows, w_in, w_out)), 0, 1)

    def combine_one(packed):
        image, returned, cotan = packed
        dispatch, combine = weights(image)
        combine_b = combine.astype(jnp.bfloat16)
        mixed = jnp.dot(combine_b, returned, preferred_element_type=jnp.float32).astype(jnp.bfloat16)
        d_out = jnp.dot(combine_b.T, cotan, preferred_element_type=jnp.float32).astype(jnp.bfloat16)
        d_combine = jnp.dot(cotan, returned.T, preferred_element_type=jnp.float32)
        d_logit_c = combine * (d_combine - lax.optimization_barrier(jnp.sum(combine * d_combine, axis=1, keepdims=True)))
        return (mixed, d_out, d_logit_c)
    mixed, d_slot_out, d_logit_c = lax.map(combine_one, (tokens, slot_out, upstream))

    def expert_backward(packed):
        slot_row_block, grad_rows, first_w, second_w = packed
        pre_act = jnp.dot(slot_row_block, first_w, preferred_element_type=jnp.float32)
        d_act = jnp.dot(grad_rows, second_w.T, preferred_element_type=jnp.float32)
        d_pre = jax.vjp(gelu_tanh, pre_act)[1](d_act)[0].astype(jnp.bfloat16)
        return jnp.dot(d_pre, first_w.T, preferred_element_type=jnp.float32).astype(jnp.bfloat16)
    d_slot_in = jnp.swapaxes(lax.map(expert_backward, (expert_rows, jnp.swapaxes(d_slot_out, 0, 1), w_in, w_out)), 0, 1)

    def finish_one(running, packed):
        image, d_slot, d_comb_part = packed
        dispatch, unused = weights(image)
        d_dispatch = jnp.dot(image, d_slot.T, preferred_element_type=jnp.float32)
        d_logit_d = dispatch * (d_dispatch - lax.optimization_barrier(jnp.sum(dispatch * d_dispatch, axis=0, keepdims=True)))
        d_logits = (d_comb_part + d_logit_d).astype(jnp.bfloat16)
        token_part = jnp.dot(d_logits, slot_key_matrix.T, preferred_element_type=jnp.float32)
        token_part = token_part + jnp.dot(dispatch.astype(jnp.bfloat16), d_slot, preferred_element_type=jnp.float32)
        running = running + jnp.dot(d_logits.T, image, preferred_element_type=jnp.float32)
        return (running, token_part.astype(jnp.bfloat16))
    key_grad, token_grad = lax.scan(finish_one, jnp.zeros((EXPERT_COUNT, D), jnp.float32), (tokens, d_slot_in, d_logit_c))
    return (mixed, token_grad, key_grad)
```

```python
import jax
import jax.numpy as jnp
from jax import lax
from jax.experimental import pallas as pl
from jax.experimental.pallas import tpu as pltpu
from jax.sharding import PartitionSpec as P

AXES = ("group", "member")
HALVES = 2
LANES = 128
KINDS = 2
CHUNK = 512
VMEM_LIMIT = 48 * 1024 * 1024
GELU_SCALE = 0.7978845608028654
GELU_CUBIC = 0.044715


def row_dot(a, b):
    return lax.dot_general(a, b, (((1,), (0,)), ((), ())), preferred_element_type=jnp.float32)


def row_dot_t(a, b):
    return lax.dot_general(a, b, (((1,), (1,)), ((), ())), preferred_element_type=jnp.float32)


def col_dot(a, b):
    return lax.dot_general(a, b, (((0,), (0,)), ((), ())), preferred_element_type=jnp.float32)


def place(spread, kind, image, images, rows):
    peers, width = rows.shape
    per_peer = KINDS * images * HALVES
    lane_blocks = spread.shape[0]
    for half in range(HALVES):
        at = (kind * images + image) * HALVES + half
        for block in range(lane_blocks):
            first = (half * lane_blocks + block) * LANES
            spread[block, pl.ds(at, peers, stride=per_peer), :] = rows[:, first : first + LANES]


def pick(spread, kind, image, images, peers):
    per_peer = KINDS * images * HALVES
    parts = []
    for half in range(HALVES):
        at = (kind * images + image) * HALVES + half
        for block in range(spread.shape[0]):
            rows = spread[block, pl.ds(at, peers, stride=per_peer), :]
            parts.append(rows.astype(jnp.bfloat16))
    return jnp.concatenate(parts, axis=1)


def widen(spread, arrived):
    for block in range(spread.shape[0]):
        lanes = slice(block * LANES, (block + 1) * LANES)
        spread[block] = arrived[:, lanes].astype(jnp.float32)


def narrow(sent, spread):
    for block in range(spread.shape[0]):
        lanes = slice(block * LANES, (block + 1) * LANES)
        sent[:, lanes] = spread[block].astype(jnp.bfloat16)


def spread_shape(rows, part):
    return pltpu.VMEM((part // LANES, rows, LANES), jnp.float32)


def route_kernel(
    tokens_hbm, upstream_hbm, key_hbm, sent, dispatch, combine, tokens, upstream, key, spread, sems
):
    images = tokens.shape[0]
    key_copy = pltpu.make_async_copy(key_hbm, key, sems.at[2 * images])
    key_copy.start()
    copies = []
    for image in range(images):
        for place_at, (source, target) in enumerate(((tokens_hbm, tokens), (upstream_hbm, upstream))):
            copy = pltpu.make_async_copy(
                source.at[image], target.at[image], sems.at[2 * image + place_at]
            )
            copy.start()
            copies.append(copy)
    key_copy.wait()
    for image in range(images):
        copies[2 * image].wait()
        logits = row_dot(tokens[image], key[...])
        by_token = jnp.exp(logits - jnp.max(logits, axis=0, keepdims=True))
        by_token = by_token / jnp.sum(by_token, axis=0, keepdims=True)
        dispatch[image] = by_token
        slot_in = col_dot(by_token.astype(jnp.bfloat16), tokens[image])
        place(spread, 0, image, images, slot_in)
        by_slot = jnp.exp(logits - jnp.max(logits, axis=1, keepdims=True))
        by_slot = by_slot / jnp.sum(by_slot, axis=1, keepdims=True)
        combine[image] = by_slot
        copies[2 * image + 1].wait()
        d_slot_out = col_dot(by_slot.astype(jnp.bfloat16), upstream[image])
        place(spread, 1, image, images, d_slot_out)
    narrow(sent, spread)


def route(tokens, upstream, slot_key_matrix):
    images, patches, width = tokens.shape
    slots = slot_key_matrix.shape[1]
    rows = slots * KINDS * images * HALVES
    part = width // HALVES
    return pl.pallas_call(
        route_kernel,
        out_shape=(
            jax.ShapeDtypeStruct((rows, part), jnp.bfloat16),
            jax.ShapeDtypeStruct((images, patches, slots), jnp.float32),
            jax.ShapeDtypeStruct((images, patches, slots), jnp.float32),
        ),
        in_specs=[pl.BlockSpec(memory_space=pl.ANY)] * 3,
        out_specs=(pl.BlockSpec(memory_space=pltpu.VMEM),) * 3,
        scratch_shapes=[
            pltpu.VMEM(tokens.shape, tokens.dtype),
            pltpu.VMEM(upstream.shape, upstream.dtype),
            pltpu.VMEM(slot_key_matrix.shape, slot_key_matrix.dtype),
            spread_shape(rows, part),
            pltpu.SemaphoreType.DMA((2 * images + 1,)),
        ],
        compiler_params=pltpu.CompilerParams(vmem_limit_bytes=VMEM_LIMIT),
        name="route",
    )(tokens, upstream, slot_key_matrix)


def expert_kernel(
    images, arrived, w_in_hbm, w_out_hbm, sent, w_in, w_out, spread, rows_in, rows_grad, out, back, sems
):
    steps, width, chunk = w_in.shape
    peers = arrived.shape[0] // (KINDS * images * HALVES)

    def weight_copies(step):
        at = pl.multiple_of(step * chunk, chunk)
        return (
            pltpu.make_async_copy(
                w_in_hbm.at[0, :, pl.ds(at, chunk)], w_in.at[step], sems.at[0, step]
            ),
            pltpu.make_async_copy(
                w_out_hbm.at[0, pl.ds(at, chunk), :], w_out.at[step], sems.at[1, step]
            ),
        )

    def begin(step, carry):
        for copy in weight_copies(step):
            copy.start()
        return carry

    lax.fori_loop(0, steps, begin, 0)
    widen(spread, arrived)
    for image in range(images):
        rows = pl.ds(image * peers, peers)
        rows_in[rows, :] = pick(spread, 0, image, images, peers)
        rows_grad[rows, :] = pick(spread, 1, image, images, peers)
    out[...] = jnp.zeros_like(out)
    back[...] = jnp.zeros_like(back)

    def one(step, carry):
        for copy in weight_copies(step):
            copy.wait()
        pre = row_dot(rows_in[...], w_in[step])
        square = pre * pre
        tanh = jnp.tanh(GELU_SCALE * (pre * (1.0 + GELU_CUBIC * square)))
        gate = 0.5 * (1.0 + tanh)
        activated = (pre * gate).astype(jnp.bfloat16)
        slope = gate + 0.5 * pre * (1.0 - tanh * tanh) * (
            GELU_SCALE * (1.0 + 3.0 * GELU_CUBIC * square)
        )
        out[...] += row_dot(activated, w_out[step])
        d_act = row_dot_t(rows_grad[...], w_out[step])
        d_pre = (d_act * slope).astype(jnp.bfloat16)
        back[...] += row_dot_t(d_pre, w_in[step])
        return carry

    lax.fori_loop(0, steps, one, 0)
    for image in range(images):
        rows = pl.ds(image * peers, peers)
        place(spread, 0, image, images, out[rows, :])
        place(spread, 1, image, images, back[rows, :])
    narrow(sent, spread)


def expert(arrived, w_in, w_out, images):
    _, width, hidden = w_in.shape
    steps = hidden // CHUNK
    rows = arrived.shape[0] // (KINDS * HALVES)

    def body(*refs):
        expert_kernel(images, *refs)

    return pl.pallas_call(
        body,
        out_shape=jax.ShapeDtypeStruct(arrived.shape, jnp.bfloat16),
        in_specs=[
            pl.BlockSpec(memory_space=pltpu.VMEM),
            pl.BlockSpec(memory_space=pl.ANY),
            pl.BlockSpec(memory_space=pl.ANY),
        ],
        out_specs=pl.BlockSpec(memory_space=pltpu.VMEM),
        scratch_shapes=[
            pltpu.VMEM((steps, width, CHUNK), w_in.dtype),
            pltpu.VMEM((steps, CHUNK, width), w_out.dtype),
            spread_shape(*arrived.shape),
            pltpu.VMEM((rows, width), jnp.bfloat16),
            pltpu.VMEM((rows, width), jnp.bfloat16),
            pltpu.VMEM((rows, width), jnp.float32),
            pltpu.VMEM((rows, width), jnp.float32),
            pltpu.SemaphoreType.DMA((2, steps)),
        ],
        compiler_params=pltpu.CompilerParams(vmem_limit_bytes=VMEM_LIMIT),
        name="expert",
    )(arrived, w_in, w_out)


def logit_grad_kernel(
    arrived, tokens, upstream, dispatch, combine, d_logits, key_part, spread, spread_key
):
    images, patches, width = tokens.shape
    slots = dispatch.shape[2]
    widen(spread, arrived)
    total = jnp.zeros((slots, width), jnp.float32)
    for image in range(images):
        returned = pick(spread, 0, image, images, slots)
        d_slot_in = pick(spread, 1, image, images, slots)
        d_combine = row_dot_t(upstream[image], returned)
        by_slot = combine[image]
        both = by_slot * (d_combine - jnp.sum(by_slot * d_combine, axis=1, keepdims=True))
        d_dispatch = row_dot_t(tokens[image], d_slot_in)
        by_token = dispatch[image]
        both += by_token * (d_dispatch - jnp.sum(by_token * d_dispatch, axis=0, keepdims=True))
        both = both.astype(jnp.bfloat16)
        d_logits[image] = both
        total += col_dot(both, tokens[image])
    lane_blocks = spread_key.shape[0]
    for half in range(HALVES):
        for block in range(lane_blocks):
            first = (half * lane_blocks + block) * LANES
            lanes = total[:, first : first + LANES]
            spread_key[block, pl.ds(half, slots, stride=HALVES), :] = lanes
    narrow(key_part, spread_key)


def logit_grad(arrived, tokens, upstream, dispatch, combine):
    images, patches, width = tokens.shape
    slots = dispatch.shape[2]
    key_shape = (slots * HALVES, width // HALVES)
    return pl.pallas_call(
        logit_grad_kernel,
        out_shape=(
            jax.ShapeDtypeStruct(dispatch.shape, jnp.bfloat16),
            jax.ShapeDtypeStruct(key_shape, jnp.bfloat16),
        ),
        in_specs=[pl.BlockSpec(memory_space=pltpu.VMEM)] * 5,
        out_specs=(pl.BlockSpec(memory_space=pltpu.VMEM),) * 2,
        scratch_shapes=[
            spread_shape(*arrived.shape),
            spread_shape(*key_shape),
        ],
        compiler_params=pltpu.CompilerParams(vmem_limit_bytes=VMEM_LIMIT),
        name="logit_grad",
    )(arrived, tokens, upstream, dispatch, combine)


def finish_kernel(arrived, dispatch, combine, d_logits, key, mixed, token_grad, spread):
    images, patches, slots = dispatch.shape
    widen(spread, arrived)
    for image in range(images):
        returned = pick(spread, 0, image, images, slots)
        mixed[image] = row_dot(combine[image].astype(jnp.bfloat16), returned).astype(jnp.bfloat16)
        d_slot_in = pick(spread, 1, image, images, slots)
        grad = row_dot_t(d_logits[image], key[...])
        grad += row_dot(dispatch[image].astype(jnp.bfloat16), d_slot_in)
        token_grad[image] = grad.astype(jnp.bfloat16)


def finish(arrived, dispatch, combine, d_logits, slot_key_matrix):
    images, patches, slots = dispatch.shape
    width = slot_key_matrix.shape[0]
    shape = jax.ShapeDtypeStruct((images, patches, width), jnp.bfloat16)
    return pl.pallas_call(
        finish_kernel,
        out_shape=(shape, shape),
        in_specs=[pl.BlockSpec(memory_space=pltpu.VMEM)] * 5,
        out_specs=(pl.BlockSpec(memory_space=pltpu.VMEM),) * 2,
        scratch_shapes=[spread_shape(*arrived.shape)],
        compiler_params=pltpu.CompilerParams(vmem_limit_bytes=VMEM_LIMIT),
        name="finish",
    )(arrived, dispatch, combine, d_logits, slot_key_matrix)


def exchange(rows, peers):
    blocks = rows.reshape(peers, -1, rows.shape[1])
    blocks = lax.all_to_all(blocks, AXES, split_axis=0, concat_axis=0, tiled=True)
    return blocks.reshape(rows.shape)


def shards(tokens, slot_key_matrix, w_in, w_out, upstream):
    images, patches, width = tokens.shape
    slots = slot_key_matrix.shape[1]
    sent, dispatch, combine = route(tokens, upstream, slot_key_matrix)
    arrived = exchange(sent, slots)
    answered = expert(arrived, w_in, w_out, images)
    returned = exchange(answered, slots)
    d_logits, key_part = logit_grad(returned, tokens, upstream, dispatch, combine)
    key_terms = exchange(key_part, slots)
    mixed, token_grad = finish(returned, dispatch, combine, d_logits, slot_key_matrix)
    key_grad = jnp.sum(key_terms.reshape(slots, 1, width).astype(jnp.float32), axis=0)
    return (mixed, token_grad, key_grad)


def solution(mesh):
    in_specs = (
        P(AXES, None, None),
        P(),
        P(AXES, None, None),
        P(AXES, None, None),
        P(AXES, None, None),
    )
    out_specs = (P(AXES, None, None), P(AXES, None, None), P(AXES, None))
    return jax.shard_map(shards, mesh=mesh, in_specs=in_specs, out_specs=out_specs, check_vma=False)
```

```python
import jax
import jax.numpy as jnp
from jax import lax
from jax.experimental import pallas as pl
from jax.experimental.pallas import tpu as pltpu
from jax.sharding import PartitionSpec as P

AXES = ("group", "member")
HALVES = 2
LANES = 128
LOAD_PARTS = 1
KINDS = 2
VMEM_LIMIT = 16 * 1024 * 1024
EXPERT_VMEM = 28 * 1024 * 1024
GELU_SCALE = 0.7978845608028654
GELU_CUBIC = 0.044715


def row_dot(a, b):
    return lax.dot_general(a, b, (((1,), (0,)), ((), ())), preferred_element_type=jnp.float32)


def row_dot_t(a, b):
    return lax.dot_general(a, b, (((1,), (1,)), ((), ())), preferred_element_type=jnp.float32)


def col_dot(a, b):
    return lax.dot_general(a, b, (((0,), (0,)), ((), ())), preferred_element_type=jnp.float32)


def place(spread, kind, image, images, rows):
    peers, width = rows.shape
    per_peer = KINDS * images * HALVES
    lane_blocks = spread.shape[0]
    for half in range(HALVES):
        at = (kind * images + image) * HALVES + half
        for block in range(lane_blocks):
            first = (half * lane_blocks + block) * LANES
            spread[block, pl.ds(at, peers, stride=per_peer), :] = rows[:, first : first + LANES]


def pick(spread, kind, image, images, peers):
    per_peer = KINDS * images * HALVES
    parts = []
    for half in range(HALVES):
        at = (kind * images + image) * HALVES + half
        for block in range(spread.shape[0]):
            rows = spread[block, pl.ds(at, peers, stride=per_peer), :]
            parts.append(rows.astype(jnp.bfloat16))
    return jnp.concatenate(parts, axis=1)


def widen(spread, arrived):
    for block in range(spread.shape[0]):
        lanes = slice(block * LANES, (block + 1) * LANES)
        spread[block] = arrived[:, lanes].astype(jnp.float32)


def narrow(sent, spread):
    for block in range(spread.shape[0]):
        lanes = slice(block * LANES, (block + 1) * LANES)
        sent[:, lanes] = spread[block].astype(jnp.bfloat16)


def spread_shape(rows, part):
    return pltpu.VMEM((part // LANES, rows, LANES), jnp.float32)


def route_kernel(
    tokens_hbm, upstream_hbm, key_hbm, sent, dispatch, combine, tokens, upstream, key, spread, sems
):
    images = tokens.shape[0]
    key_copy = pltpu.make_async_copy(key_hbm, key, sems.at[2 * images])
    key_copy.start()
    copies = []
    for image in range(images):
        for place_at, (source, target) in enumerate(((tokens_hbm, tokens), (upstream_hbm, upstream))):
            copy = pltpu.make_async_copy(
                source.at[image], target.at[image], sems.at[2 * image + place_at]
            )
            copy.start()
            copies.append(copy)
    key_copy.wait()
    for image in range(images):
        copies[2 * image].wait()
        logits = row_dot(tokens[image], key[...])
        by_token = jnp.exp(logits - jnp.max(logits, axis=0, keepdims=True))
        by_token = by_token / jnp.sum(by_token, axis=0, keepdims=True)
        dispatch[image] = by_token
        slot_in = col_dot(by_token.astype(jnp.bfloat16), tokens[image])
        place(spread, 0, image, images, slot_in)
        by_slot = jnp.exp(logits - jnp.max(logits, axis=1, keepdims=True))
        by_slot = by_slot / jnp.sum(by_slot, axis=1, keepdims=True)
        combine[image] = by_slot
        copies[2 * image + 1].wait()
        d_slot_out = col_dot(by_slot.astype(jnp.bfloat16), upstream[image])
        place(spread, 1, image, images, d_slot_out)
    narrow(sent, spread)


def route(tokens, upstream, slot_key_matrix):
    images, patches, width = tokens.shape
    slots = slot_key_matrix.shape[1]
    rows = slots * KINDS * images * HALVES
    part = width // HALVES
    return pl.pallas_call(
        route_kernel,
        out_shape=(
            jax.ShapeDtypeStruct((rows, part), jnp.bfloat16),
            jax.ShapeDtypeStruct((images, patches, slots), jnp.float32),
            jax.ShapeDtypeStruct((images, patches, slots), jnp.float32),
        ),
        in_specs=[pl.BlockSpec(memory_space=pltpu.HBM)] * 3,
        out_specs=(pl.BlockSpec(memory_space=pltpu.VMEM),) * 3,
        scratch_shapes=[
            pltpu.VMEM(tokens.shape, tokens.dtype),
            pltpu.VMEM(upstream.shape, upstream.dtype),
            pltpu.VMEM(slot_key_matrix.shape, slot_key_matrix.dtype),
            spread_shape(rows, part),
            pltpu.SemaphoreType.DMA((2 * images + 1,)),
        ],
        compiler_params=pltpu.CompilerParams(vmem_limit_bytes=VMEM_LIMIT),
        name="route",
    )(*(pltpu.with_memory_space_constraint(x, pltpu.HBM) for x in (tokens, upstream, slot_key_matrix)))


def hold_kernel(rows, out):
    del rows, out


def hold(rows):
    return pl.pallas_call(
        hold_kernel,
        out_shape=jax.ShapeDtypeStruct(rows.shape, rows.dtype),
        in_specs=[pl.BlockSpec(memory_space=pl.ANY)],
        out_specs=pl.BlockSpec(memory_space=pl.ANY),
        input_output_aliases={0: 0},
        cost_estimate=pl.CostEstimate(flops=10**9, bytes_accessed=10**8, transcendentals=10**6),
        compiler_params=pltpu.CompilerParams(vmem_limit_bytes=1024 * 1024),
        name="hold",
    )(rows)


def expert_kernel(images, arrived, w_in, w_out_hbm, sent, w_out, spread, answers, sems):
    peers = arrived.shape[0] // (KINDS * images * HALVES)
    hidden = w_out.shape[0] // LOAD_PARTS
    copies = []
    for at in range(LOAD_PARTS):
        part = pl.ds(at * hidden, hidden)
        copies.append(pltpu.make_async_copy(w_out_hbm.at[0, part], w_out.at[part], sems.at[at]))
    for copy in copies:
        copy.start()
    widen(spread, arrived)

    def rows_of(kind):
        return jnp.concatenate(
            [pick(spread, kind, image, images, peers) for image in range(images)], axis=0
        )

    def answer(kind, rows):
        for image in range(images):
            place(answers, kind, image, images, rows[image * peers : (image + 1) * peers])

    pre = row_dot(rows_of(0), w_in[0])
    rows_grad = rows_of(1)
    d_act = []
    for at, copy in enumerate(copies):
        copy.wait()
        d_act.append(row_dot_t(rows_grad, w_out[at * hidden : (at + 1) * hidden]))
    d_act = jnp.concatenate(d_act, axis=1)
    square = pre * pre
    tanh = jnp.tanh(GELU_SCALE * (pre * (1.0 + GELU_CUBIC * square)))
    gate = 0.5 * (1.0 + tanh)
    activated = (pre * gate).astype(jnp.bfloat16)
    slope = gate + 0.5 * pre * (1.0 - tanh * tanh) * (
        GELU_SCALE * (1.0 + 3.0 * GELU_CUBIC * square)
    )
    d_pre = (d_act * slope).astype(jnp.bfloat16)
    answer(0, row_dot(activated, w_out[...]))
    answer(1, row_dot_t(d_pre, w_in[0]))
    narrow(sent, answers)


def expert(arrived, w_in, w_out, images):
    def body(*refs):
        expert_kernel(images, *refs)

    return pl.pallas_call(
        body,
        out_shape=jax.ShapeDtypeStruct(arrived.shape, jnp.bfloat16),
        in_specs=[pl.BlockSpec(memory_space=pltpu.VMEM)] * 2
        + [pl.BlockSpec(memory_space=pltpu.HBM)],
        out_specs=pl.BlockSpec(memory_space=pltpu.VMEM),
        scratch_shapes=[
            pltpu.VMEM(w_out.shape[1:], w_out.dtype),
            spread_shape(*arrived.shape),
            spread_shape(*arrived.shape),
            pltpu.SemaphoreType.DMA((LOAD_PARTS,)),
        ],
        compiler_params=pltpu.CompilerParams(vmem_limit_bytes=EXPERT_VMEM),
        name="expert",
    )(arrived, w_in, pltpu.with_memory_space_constraint(w_out, pltpu.HBM))


def logit_grad_kernel(
    arrived, tokens, upstream, dispatch, combine, d_logits, key_part, spread
):
    images, patches, width = tokens.shape
    slots = dispatch.shape[2]
    widen(spread, arrived)
    total = jnp.zeros((slots, width), jnp.float32)
    for image in range(images):
        returned = pick(spread, 0, image, images, slots)
        d_slot_in = pick(spread, 1, image, images, slots)
        d_combine = row_dot_t(upstream[image], returned)
        by_slot = combine[image]
        both = by_slot * (d_combine - jnp.sum(by_slot * d_combine, axis=1, keepdims=True))
        d_dispatch = row_dot_t(tokens[image], d_slot_in)
        by_token = dispatch[image]
        both += by_token * (d_dispatch - jnp.sum(by_token * d_dispatch, axis=0, keepdims=True))
        both = both.astype(jnp.bfloat16)
        d_logits[image] = both
        total += col_dot(both, tokens[image])
    part = width // HALVES
    for half in range(HALVES):
        lanes = total[:, half * part : (half + 1) * part]
        key_part[:, half, :] = lanes.astype(jnp.bfloat16)


def logit_grad(arrived, tokens, upstream, dispatch, combine):
    images, patches, width = tokens.shape
    slots = dispatch.shape[2]
    key_shape = (slots, HALVES, width // HALVES)
    return pl.pallas_call(
        logit_grad_kernel,
        out_shape=(
            jax.ShapeDtypeStruct(dispatch.shape, jnp.bfloat16),
            jax.ShapeDtypeStruct(key_shape, jnp.bfloat16),
        ),
        in_specs=[pl.BlockSpec(memory_space=pltpu.VMEM)] * 5,
        out_specs=(pl.BlockSpec(memory_space=pltpu.VMEM),) * 2,
        scratch_shapes=[spread_shape(*arrived.shape)],
        compiler_params=pltpu.CompilerParams(vmem_limit_bytes=VMEM_LIMIT),
        name="logit_grad",
    )(arrived, tokens, upstream, dispatch, combine)


def finish_kernel(arrived, dispatch, combine, d_logits, key, mixed, token_grad, spread):
    images, patches, slots = dispatch.shape
    widen(spread, arrived)
    for image in range(images):
        returned = pick(spread, 0, image, images, slots)
        mixed[image] = row_dot(combine[image].astype(jnp.bfloat16), returned).astype(jnp.bfloat16)
        d_slot_in = pick(spread, 1, image, images, slots)
        grad = row_dot_t(d_logits[image], key[...])
        grad += row_dot(dispatch[image].astype(jnp.bfloat16), d_slot_in)
        token_grad[image] = grad.astype(jnp.bfloat16)


def finish(arrived, dispatch, combine, d_logits, slot_key_matrix):
    images, patches, slots = dispatch.shape
    width = slot_key_matrix.shape[0]
    shape = jax.ShapeDtypeStruct((images, patches, width), jnp.bfloat16)
    return pl.pallas_call(
        finish_kernel,
        out_shape=(shape, shape),
        in_specs=[pl.BlockSpec(memory_space=pltpu.VMEM)] * 5,
        out_specs=(pl.BlockSpec(memory_space=pltpu.VMEM),) * 2,
        scratch_shapes=[spread_shape(*arrived.shape)],
        compiler_params=pltpu.CompilerParams(vmem_limit_bytes=VMEM_LIMIT),
        name="finish",
    )(arrived, dispatch, combine, d_logits, slot_key_matrix)


def key_sum_kernel(terms, total):
    part = terms.shape[2]
    own = jnp.sum(terms[...].astype(jnp.float32), axis=0)
    for half in range(HALVES):
        total[:, half * part : (half + 1) * part] = own[half : half + 1]


def key_sum(terms):
    return pl.pallas_call(
        key_sum_kernel,
        out_shape=jax.ShapeDtypeStruct((1, terms.shape[1] * terms.shape[2]), jnp.float32),
        in_specs=[pl.BlockSpec(memory_space=pltpu.VMEM)],
        out_specs=pl.BlockSpec(memory_space=pltpu.VMEM),
        compiler_params=pltpu.CompilerParams(vmem_limit_bytes=VMEM_LIMIT),
        name="key_sum",
    )(terms)


def exchange(blocks):
    return lax.all_to_all(blocks, AXES, split_axis=0, concat_axis=0, tiled=True)


def exchange_rows(rows, peers):
    return exchange(rows.reshape(peers, -1, rows.shape[1])).reshape(rows.shape)


def shards(tokens, slot_key_matrix, w_in, w_out, upstream):
    images, patches, width = tokens.shape
    slots = slot_key_matrix.shape[1]
    sent, dispatch, combine = route(tokens, upstream, slot_key_matrix)
    arrived = exchange_rows(hold(sent), slots)
    answered = expert(arrived, w_in, w_out, images)
    returned = exchange_rows(answered, slots)
    d_logits, key_part = logit_grad(returned, tokens, upstream, dispatch, combine)
    key_terms = exchange(key_part)
    mixed, token_grad = finish(returned, dispatch, combine, d_logits, slot_key_matrix)
    key_grad = key_sum(key_terms)
    return (mixed, token_grad, key_grad)


def solution(mesh):
    in_specs = (
        P(AXES, None, None),
        P(),
        P(AXES, None, None),
        P(AXES, None, None),
        P(AXES, None, None),
    )
    out_specs = (P(AXES, None, None), P(AXES, None, None), P(AXES, None))
    return jax.shard_map(shards, mesh=mesh, in_specs=in_specs, out_specs=out_specs, check_vma=False)
```

```python
import functools
import math

import jax
import jax.numpy as jnp
from jax import lax
from jax.experimental import pallas as pl
from jax.experimental.pallas import tpu as pltpu
from jax.sharding import PartitionSpec as P

AXES = ("group", "member")
EXCHANGE_AXES = ("member", "group")
HALVES = 2
LANES = 128
KINDS = 2
VMEM_LIMIT = 16 * 1024 * 1024
EXPERT_VMEM = 28 * 1024 * 1024
GELU_SCALE = 0.7978845608028654
GELU_CUBIC = 0.044715


def row_dot(a, b):
    return lax.dot_general(a, b, (((1,), (0,)), ((), ())), preferred_element_type=jnp.float32)


def row_dot_t(a, b):
    return lax.dot_general(a, b, (((1,), (1,)), ((), ())), preferred_element_type=jnp.float32)


def col_dot(a, b):
    return lax.dot_general(a, b, (((0,), (0,)), ((), ())), preferred_element_type=jnp.float32)


def place(spread, kind, image, images, rows):
    peers, width = rows.shape
    per_peer = KINDS * images * HALVES
    lane_blocks = spread.shape[0]
    for half in range(HALVES):
        at = (kind * images + image) * HALVES + half
        for block in range(lane_blocks):
            first = (half * lane_blocks + block) * LANES
            spread[block, pl.ds(at, peers, stride=per_peer), :] = rows[:, first : first + LANES]


def pick(spread, kind, image, images, peers):
    per_peer = KINDS * images * HALVES
    parts = []
    for half in range(HALVES):
        at = (kind * images + image) * HALVES + half
        for block in range(spread.shape[0]):
            rows = spread[block, pl.ds(at, peers, stride=per_peer), :]
            parts.append(rows.astype(jnp.bfloat16))
    return jnp.concatenate(parts, axis=1)


def widen(spread, arrived, groups):
    rows = spread.shape[1] // groups
    for block in range(spread.shape[0]):
        lanes = slice(block * LANES, (block + 1) * LANES)
        for group in range(groups):
            own = arrived[:, group, :, lanes].astype(jnp.float32)
            spread[block, group * rows : (group + 1) * rows, :] = own.reshape(rows, LANES)


def narrow(sent, spread, groups):
    rows = spread.shape[1] // groups
    per_peer = sent.shape[2]
    for block in range(spread.shape[0]):
        lanes = slice(block * LANES, (block + 1) * LANES)
        for group in range(groups):
            own = spread[block, group * rows : (group + 1) * rows, :]
            sent[:, group, :, lanes] = own.reshape(-1, per_peer, LANES).astype(jnp.bfloat16)


def spread_shape(rows, part):
    return pltpu.VMEM((part // LANES, rows, LANES), jnp.float32)


def route_kernel(
    groups,
    tokens_hbm,
    upstream_hbm,
    key_hbm,
    weight_hbm,
    sent,
    dispatch,
    combine,
    weight,
    tokens,
    upstream,
    key,
    spread,
    sems,
):
    images = tokens.shape[0]
    key_copy = pltpu.make_async_copy(key_hbm, key, sems.at[2 * images])
    key_copy.start()
    copies = []
    for place_at, (source, target) in enumerate(((tokens_hbm, tokens), (upstream_hbm, upstream))):
        for image in range(images):
            copy = pltpu.make_async_copy(
                source.at[image], target.at[image], sems.at[2 * image + place_at]
            )
            copy.start()
            copies.append(copy)
    weight_copy = pltpu.make_async_copy(weight_hbm.at[0], weight, sems.at[2 * images + 1])
    weight_copy.start()
    key_copy.wait()
    for image in range(images):
        copies[image].wait()
    slot_weights = []
    for image in range(images):
        logits = row_dot(tokens[image], key[...])
        by_token = jnp.exp(logits - jnp.max(logits, axis=0, keepdims=True))
        by_token = by_token / jnp.sum(by_token, axis=0, keepdims=True)
        dispatch[image] = by_token
        by_slot = jnp.exp(logits - jnp.max(logits, axis=1, keepdims=True))
        by_slot = by_slot / jnp.sum(by_slot, axis=1, keepdims=True)
        combine[image] = by_slot
        slot_weights.append(by_slot.astype(jnp.bfloat16))
        slot_in = col_dot(by_token.astype(jnp.bfloat16), tokens[image])
        place(spread, 0, image, images, slot_in)
    for image in range(images):
        copies[images + image].wait()
    for image in range(images):
        d_slot_out = col_dot(slot_weights[image], upstream[image])
        place(spread, 1, image, images, d_slot_out)
    narrow(sent, spread, groups)
    weight_copy.wait()


def route(tokens, upstream, slot_key_matrix, weight, groups):
    images, patches, width = tokens.shape
    slots = slot_key_matrix.shape[1]
    per_peer = KINDS * images * HALVES
    rows = slots * per_peer
    part = width // HALVES
    return pl.pallas_call(
        functools.partial(route_kernel, groups),
        out_shape=(
            jax.ShapeDtypeStruct((slots // groups, groups, per_peer, part), jnp.bfloat16),
            jax.ShapeDtypeStruct((images, patches, slots), jnp.float32),
            jax.ShapeDtypeStruct((images, patches, slots), jnp.float32),
            pltpu.VMEM(weight.shape[1:], weight.dtype),
        ),
        in_specs=[pl.BlockSpec(memory_space=pltpu.HBM)] * 4,
        out_specs=(pl.BlockSpec(memory_space=pltpu.VMEM),) * 4,
        scratch_shapes=[
            pltpu.VMEM(tokens.shape, tokens.dtype),
            pltpu.VMEM(upstream.shape, upstream.dtype),
            pltpu.VMEM(slot_key_matrix.shape, slot_key_matrix.dtype),
            spread_shape(rows, part),
            pltpu.SemaphoreType.DMA((2 * images + 2,)),
        ],
        compiler_params=pltpu.CompilerParams(vmem_limit_bytes=VMEM_LIMIT),
        name="route",
    )(*(pltpu.with_memory_space_constraint(x, pltpu.HBM) for x in (tokens, upstream, slot_key_matrix, weight)))


def hold_kernel(rows, out):
    del rows, out


def hold(rows):
    return pl.pallas_call(
        hold_kernel,
        out_shape=jax.ShapeDtypeStruct(rows.shape, rows.dtype),
        in_specs=[pl.BlockSpec(memory_space=pl.ANY)],
        out_specs=pl.BlockSpec(memory_space=pl.ANY),
        input_output_aliases={0: 0},
        cost_estimate=pl.CostEstimate(flops=10**9, bytes_accessed=10**8, transcendentals=10**6),
        compiler_params=pltpu.CompilerParams(vmem_limit_bytes=1024 * 1024),
        name="hold",
    )(rows)


def expert_kernel(images, arrived, w_in, w_out, sent, spread, answers):
    peers = arrived.shape[0] // (KINDS * images * HALVES)
    for block in range(spread.shape[0]):
        lanes = slice(block * LANES, (block + 1) * LANES)
        spread[block] = arrived[:, lanes].astype(jnp.float32)

    def rows_of(kind):
        return jnp.concatenate(
            [pick(spread, kind, image, images, peers) for image in range(images)], axis=0
        )

    def answer(kind, rows):
        for image in range(images):
            place(answers, kind, image, images, rows[image * peers : (image + 1) * peers])

    pre = row_dot(rows_of(0), w_in[0])
    square = pre * pre
    tanh = jnp.tanh(GELU_SCALE * (pre * (1.0 + GELU_CUBIC * square)))
    gate = 0.5 * (1.0 + tanh)
    activated = (pre * gate).astype(jnp.bfloat16)
    slope = gate + 0.5 * pre * (1.0 - tanh * tanh) * (
        GELU_SCALE * (1.0 + 3.0 * GELU_CUBIC * square)
    )
    d_act = row_dot_t(rows_of(1), w_out[...])
    d_pre = (d_act * slope).astype(jnp.bfloat16)
    answer(0, row_dot(activated, w_out[...]))
    answer(1, row_dot_t(d_pre, w_in[0]))
    for block in range(spread.shape[0]):
        lanes = slice(block * LANES, (block + 1) * LANES)
        sent[:, lanes] = answers[block].astype(jnp.bfloat16)


def expert(arrived, w_in, w_out, images):
    def body(*refs):
        expert_kernel(images, *refs)

    return pl.pallas_call(
        body,
        out_shape=jax.ShapeDtypeStruct(arrived.shape, jnp.bfloat16),
        in_specs=[pl.BlockSpec(memory_space=pltpu.VMEM)] * 3,
        out_specs=pl.BlockSpec(memory_space=pltpu.VMEM),
        scratch_shapes=[spread_shape(*arrived.shape), spread_shape(*arrived.shape)],
        compiler_params=pltpu.CompilerParams(vmem_limit_bytes=EXPERT_VMEM),
        name="expert",
    )(arrived, w_in, w_out)


def logit_grad_kernel(
    groups, arrived, tokens, upstream, dispatch, combine, d_logits, key_part, spread
):
    images, patches, width = tokens.shape
    slots = dispatch.shape[2]
    widen(spread, arrived, groups)
    total = jnp.zeros((slots, width), jnp.float32)
    for image in range(images):
        returned = pick(spread, 0, image, images, slots)
        d_slot_in = pick(spread, 1, image, images, slots)
        d_combine = row_dot_t(upstream[image], returned)
        by_slot = combine[image]
        both = by_slot * (d_combine - jnp.sum(by_slot * d_combine, axis=1, keepdims=True))
        d_dispatch = row_dot_t(tokens[image], d_slot_in)
        by_token = dispatch[image]
        both += by_token * (d_dispatch - jnp.sum(by_token * d_dispatch, axis=0, keepdims=True))
        both = both.astype(jnp.bfloat16)
        d_logits[image] = both
        total += col_dot(both, tokens[image])
    part = width // HALVES
    members = slots // groups
    for half in range(HALVES):
        lanes = total[:, half * part : (half + 1) * part]
        for group in range(groups):
            rows = lanes[group * members : (group + 1) * members]
            key_part[:, group, half, :] = rows.astype(jnp.bfloat16)


def logit_grad(arrived, tokens, upstream, dispatch, combine, groups):
    images, patches, width = tokens.shape
    slots = dispatch.shape[2]
    key_shape = (slots // groups, groups, HALVES, width // HALVES)
    return pl.pallas_call(
        functools.partial(logit_grad_kernel, groups),
        out_shape=(
            jax.ShapeDtypeStruct(dispatch.shape, jnp.bfloat16),
            jax.ShapeDtypeStruct(key_shape, jnp.bfloat16),
        ),
        in_specs=[pl.BlockSpec(memory_space=pltpu.VMEM)] * 5,
        out_specs=(pl.BlockSpec(memory_space=pltpu.VMEM),) * 2,
        scratch_shapes=[spread_shape(math.prod(arrived.shape[:-1]), arrived.shape[-1])],
        compiler_params=pltpu.CompilerParams(vmem_limit_bytes=VMEM_LIMIT),
        name="logit_grad",
    )(arrived, tokens, upstream, dispatch, combine)


def finish_kernel(groups, arrived, dispatch, combine, d_logits, key, mixed, token_grad, spread):
    images, patches, slots = dispatch.shape
    widen(spread, arrived, groups)
    for image in range(images):
        returned = pick(spread, 0, image, images, slots)
        mixed[image] = row_dot(combine[image].astype(jnp.bfloat16), returned).astype(jnp.bfloat16)
        d_slot_in = pick(spread, 1, image, images, slots)
        grad = row_dot_t(d_logits[image], key[...])
        grad += row_dot(dispatch[image].astype(jnp.bfloat16), d_slot_in)
        token_grad[image] = grad.astype(jnp.bfloat16)


def finish(arrived, dispatch, combine, d_logits, slot_key_matrix, groups):
    images, patches, slots = dispatch.shape
    width = slot_key_matrix.shape[0]
    shape = jax.ShapeDtypeStruct((images, patches, width), jnp.bfloat16)
    return pl.pallas_call(
        functools.partial(finish_kernel, groups),
        out_shape=(shape, shape),
        in_specs=[pl.BlockSpec(memory_space=pltpu.VMEM)] * 5,
        out_specs=(pl.BlockSpec(memory_space=pltpu.VMEM),) * 2,
        scratch_shapes=[spread_shape(math.prod(arrived.shape[:-1]), arrived.shape[-1])],
        compiler_params=pltpu.CompilerParams(vmem_limit_bytes=VMEM_LIMIT),
        name="finish",
    )(arrived, dispatch, combine, d_logits, slot_key_matrix)


def key_sum_kernel(terms, total):
    part = terms.shape[2]
    own = jnp.sum(terms[...].astype(jnp.float32), axis=0)
    for half in range(HALVES):
        total[:, half * part : (half + 1) * part] = own[half : half + 1]


def key_sum(terms):
    return pl.pallas_call(
        key_sum_kernel,
        out_shape=jax.ShapeDtypeStruct((1, terms.shape[1] * terms.shape[2]), jnp.float32),
        in_specs=[pl.BlockSpec(memory_space=pltpu.VMEM)],
        out_specs=pl.BlockSpec(memory_space=pltpu.VMEM),
        compiler_params=pltpu.CompilerParams(vmem_limit_bytes=VMEM_LIMIT),
        name="key_sum",
    )(terms)


def exchange(blocks):
    return lax.all_to_all(blocks, EXCHANGE_AXES, split_axis=0, concat_axis=0, tiled=True)


def shards(tokens, slot_key_matrix, w_in, w_out, upstream, groups=4):
    images, patches, width = tokens.shape
    slots = slot_key_matrix.shape[1]
    sent, dispatch, combine, w_out = route(tokens, upstream, slot_key_matrix, w_out, groups)
    by_group = sent.shape
    per_peer, part = by_group[2:]
    arrived = exchange(hold(sent).reshape(slots, per_peer, part))
    answered = expert(arrived.reshape(-1, part), w_in, w_out, images)
    returned = exchange(answered.reshape(slots, per_peer, part)).reshape(by_group)
    d_logits, key_part = logit_grad(returned, tokens, upstream, dispatch, combine, groups)
    key_terms = exchange(key_part.reshape(slots, HALVES, -1))
    mixed, token_grad = finish(returned, dispatch, combine, d_logits, slot_key_matrix, groups)
    key_grad = key_sum(key_terms)
    return (mixed, token_grad, key_grad)


def solution(mesh):
    in_specs = (
        P(AXES, None, None),
        P(),
        P(AXES, None, None),
        P(AXES, None, None),
        P(AXES, None, None),
    )
    out_specs = (P(AXES, None, None), P(AXES, None, None), P(AXES, None))
    body = functools.partial(shards, groups=mesh.shape["group"])
    return jax.shard_map(body, mesh=mesh, in_specs=in_specs, out_specs=out_specs, check_vma=False)
```

```python
import functools
import math

import jax
import jax.numpy as jnp
from jax import lax
from jax.experimental import pallas as pl
from jax.experimental.pallas import tpu as pltpu
from jax.sharding import PartitionSpec as P

AXES = ("group", "member")
EXCHANGE_AXES = ("member", "group")
HALVES = 2
LANES = 128
KINDS = 2
VMEM_LIMIT = 16 * 1024 * 1024
EXPERT_VMEM = 28 * 1024 * 1024
GELU_SCALE = 0.7978845608028654
GELU_CUBIC = 0.044715


def row_dot(a, b):
    return lax.dot_general(a, b, (((1,), (0,)), ((), ())), preferred_element_type=jnp.float32)


def row_dot_t(a, b):
    return lax.dot_general(a, b, (((1,), (1,)), ((), ())), preferred_element_type=jnp.float32)


def col_dot(a, b):
    return lax.dot_general(a, b, (((0,), (0,)), ((), ())), preferred_element_type=jnp.float32)


def place(spread, kind, image, images, rows):
    peers, width = rows.shape
    per_peer = KINDS * images * HALVES
    lane_blocks = spread.shape[0]
    for half in range(HALVES):
        at = (kind * images + image) * HALVES + half
        for block in range(lane_blocks):
            first = (block * HALVES + half) * LANES
            spread[block, pl.ds(at, peers, stride=per_peer), :] = rows[:, first : first + LANES]


def pick(spread, kind, image, images, peers):
    per_peer = KINDS * images * HALVES
    parts = []
    for block in range(spread.shape[0]):
        for half in range(HALVES):
            at = (kind * images + image) * HALVES + half
            rows = spread[block, pl.ds(at, peers, stride=per_peer), :]
            parts.append(rows.astype(jnp.bfloat16))
    return jnp.concatenate(parts, axis=1)


def widen(spread, arrived, groups):
    rows = spread.shape[1] // groups
    for block in range(spread.shape[0]):
        lanes = slice(block * LANES, (block + 1) * LANES)
        for group in range(groups):
            own = arrived[:, group, :, lanes].astype(jnp.float32)
            spread[block, group * rows : (group + 1) * rows, :] = own.reshape(rows, LANES)


def narrow(sent, spread, groups):
    rows = spread.shape[1] // groups
    per_peer = sent.shape[2]
    for block in range(spread.shape[0]):
        lanes = slice(block * LANES, (block + 1) * LANES)
        for group in range(groups):
            own = spread[block, group * rows : (group + 1) * rows, :]
            sent[:, group, :, lanes] = own.reshape(-1, per_peer, LANES).astype(jnp.bfloat16)


def spread_shape(rows, part):
    return pltpu.VMEM((part // LANES, rows, LANES), jnp.float32)


def route_kernel(
    groups,
    tokens_hbm,
    upstream_hbm,
    key_hbm,
    weight_hbm,
    sent,
    dispatch,
    combine,
    weight,
    tokens,
    upstream,
    key,
    spread,
    sems,
):
    images = tokens.shape[0]
    key_copy = pltpu.make_async_copy(key_hbm, key, sems.at[2 * images])
    key_copy.start()
    copies = []
    for place_at, (source, target) in enumerate(((tokens_hbm, tokens), (upstream_hbm, upstream))):
        for image in range(images):
            copy = pltpu.make_async_copy(
                source.at[image], target.at[image], sems.at[2 * image + place_at]
            )
            copy.start()
            copies.append(copy)
    weight_copy = pltpu.make_async_copy(weight_hbm.at[0], weight, sems.at[2 * images + 1])
    weight_copy.start()
    key_copy.wait()
    for image in range(images):
        copies[image].wait()
    slot_weights = []
    patches, width = tokens.shape[1:]
    all_logits = row_dot(tokens[...].reshape(images * patches, width), key[...])
    for image in range(images):
        logits = all_logits[image * patches : (image + 1) * patches]
        by_token = jnp.exp(logits - jnp.max(logits, axis=0, keepdims=True))
        by_token = by_token / jnp.sum(by_token, axis=0, keepdims=True)
        dispatch[image] = by_token
        by_slot = jnp.exp(logits - jnp.max(logits, axis=1, keepdims=True))
        by_slot = by_slot / jnp.sum(by_slot, axis=1, keepdims=True)
        combine[image] = by_slot
        slot_weights.append(by_slot.astype(jnp.bfloat16))
        slot_in = col_dot(by_token.astype(jnp.bfloat16), tokens[image])
        place(spread, 0, image, images, slot_in)
    for image in range(images):
        copies[images + image].wait()
    for image in range(images):
        d_slot_out = col_dot(slot_weights[image], upstream[image])
        place(spread, 1, image, images, d_slot_out)
    narrow(sent, spread, groups)
    weight_copy.wait()


def route(tokens, upstream, slot_key_matrix, weight, groups):
    images, patches, width = tokens.shape
    slots = slot_key_matrix.shape[1]
    per_peer = KINDS * images * HALVES
    rows = slots * per_peer
    part = width // HALVES
    return pl.pallas_call(
        functools.partial(route_kernel, groups),
        out_shape=(
            jax.ShapeDtypeStruct((slots // groups, groups, per_peer, part), jnp.bfloat16),
            jax.ShapeDtypeStruct((images, patches, slots), jnp.float32),
            jax.ShapeDtypeStruct((images, patches, slots), jnp.float32),
            pltpu.VMEM(weight.shape[1:], weight.dtype),
        ),
        in_specs=[pl.BlockSpec(memory_space=pltpu.HBM)] * 4,
        out_specs=(pl.BlockSpec(memory_space=pltpu.VMEM),) * 4,
        scratch_shapes=[
            pltpu.VMEM(tokens.shape, tokens.dtype),
            pltpu.VMEM(upstream.shape, upstream.dtype),
            pltpu.VMEM(slot_key_matrix.shape, slot_key_matrix.dtype),
            spread_shape(rows, part),
            pltpu.SemaphoreType.DMA((2 * images + 2,)),
        ],
        compiler_params=pltpu.CompilerParams(vmem_limit_bytes=VMEM_LIMIT),
        name="route",
    )(*(pltpu.with_memory_space_constraint(x, pltpu.HBM) for x in (tokens, upstream, slot_key_matrix, weight)))


def hold_kernel(rows, out):
    del rows, out


def hold(rows):
    return pl.pallas_call(
        hold_kernel,
        out_shape=jax.ShapeDtypeStruct(rows.shape, rows.dtype),
        in_specs=[pl.BlockSpec(memory_space=pl.ANY)],
        out_specs=pl.BlockSpec(memory_space=pl.ANY),
        input_output_aliases={0: 0},
        cost_estimate=pl.CostEstimate(flops=10**9, bytes_accessed=10**8, transcendentals=10**6),
        compiler_params=pltpu.CompilerParams(vmem_limit_bytes=1024 * 1024),
        name="hold",
    )(rows)


def expert_kernel(images, arrived, w_in, w_out, sent, spread, answers):
    peers = arrived.shape[0] // (KINDS * images * HALVES)
    for block in range(spread.shape[0]):
        lanes = slice(block * LANES, (block + 1) * LANES)
        spread[block] = arrived[:, lanes].astype(jnp.float32)

    def rows_of(kind):
        return jnp.concatenate(
            [pick(spread, kind, image, images, peers) for image in range(images)], axis=0
        )

    def answer(kind, rows, block=None):
        for image in range(images):
            own = rows[image * peers : (image + 1) * peers]
            if block is None:
                place(answers, kind, image, images, own)
            else:
                place(answers.at[pl.ds(block, 1)], kind, image, images, own)

    pre = row_dot(rows_of(0), w_in[0])
    square = pre * pre
    tanh = jnp.tanh(GELU_SCALE * (pre * (1.0 + GELU_CUBIC * square)))
    gate = 0.5 * (1.0 + tanh)
    activated = (pre * gate).astype(jnp.bfloat16)
    slope = gate + 0.5 * pre * (1.0 - tanh * tanh) * (
        GELU_SCALE * (1.0 + 3.0 * GELU_CUBIC * square)
    )
    d_act = row_dot_t(rows_of(1), w_out[...])
    d_pre = (d_act * slope).astype(jnp.bfloat16)
    answer(0, row_dot(activated, w_out[...]))
    columns = HALVES * LANES
    for block in range(spread.shape[0]):
        rows = slice(block * columns, (block + 1) * columns)
        answer(1, row_dot_t(d_pre, w_in[0, rows]), block)
        lanes = slice(block * LANES, (block + 1) * LANES)
        sent[:, lanes] = answers[block].astype(jnp.bfloat16)


def expert(arrived, w_in, w_out, images):
    def body(*refs):
        expert_kernel(images, *refs)

    return pl.pallas_call(
        body,
        out_shape=jax.ShapeDtypeStruct(arrived.shape, jnp.bfloat16),
        in_specs=[pl.BlockSpec(memory_space=pltpu.VMEM)] * 3,
        out_specs=pl.BlockSpec(memory_space=pltpu.VMEM),
        scratch_shapes=[spread_shape(*arrived.shape), spread_shape(*arrived.shape)],
        compiler_params=pltpu.CompilerParams(vmem_limit_bytes=EXPERT_VMEM),
        name="expert",
    )(arrived, w_in, w_out)


def logit_grad_kernel(
    groups, arrived, tokens, upstream, dispatch, combine, d_logits, key_part, spread
):
    images, patches, width = tokens.shape
    slots = dispatch.shape[2]
    widen(spread, arrived, groups)
    total = jnp.zeros((slots, width), jnp.float32)
    for image in range(images):
        returned = pick(spread, 0, image, images, slots)
        d_slot_in = pick(spread, 1, image, images, slots)
        d_combine = row_dot_t(upstream[image], returned)
        by_slot = combine[image]
        both = by_slot * (d_combine - jnp.sum(by_slot * d_combine, axis=1, keepdims=True))
        d_dispatch = row_dot_t(tokens[image], d_slot_in)
        by_token = dispatch[image]
        both += by_token * (d_dispatch - jnp.sum(by_token * d_dispatch, axis=0, keepdims=True))
        both = both.astype(jnp.bfloat16)
        d_logits[image] = both
        total += col_dot(both, tokens[image])
    part = width // HALVES
    members = slots // groups
    for half in range(HALVES):
        lanes = total[:, half * part : (half + 1) * part]
        for group in range(groups):
            rows = lanes[group * members : (group + 1) * members]
            key_part[:, group, half, :] = rows.astype(jnp.bfloat16)


def logit_grad(arrived, tokens, upstream, dispatch, combine, groups):
    images, patches, width = tokens.shape
    slots = dispatch.shape[2]
    key_shape = (slots // groups, groups, HALVES, width // HALVES)
    return pl.pallas_call(
        functools.partial(logit_grad_kernel, groups),
        out_shape=(
            jax.ShapeDtypeStruct(dispatch.shape, jnp.bfloat16),
            jax.ShapeDtypeStruct(key_shape, jnp.bfloat16),
        ),
        in_specs=[pl.BlockSpec(memory_space=pltpu.VMEM)] * 5,
        out_specs=(pl.BlockSpec(memory_space=pltpu.VMEM),) * 2,
        scratch_shapes=[spread_shape(math.prod(arrived.shape[:-1]), arrived.shape[-1])],
        compiler_params=pltpu.CompilerParams(vmem_limit_bytes=VMEM_LIMIT),
        name="logit_grad",
    )(arrived, tokens, upstream, dispatch, combine)


def finish_kernel(groups, arrived, dispatch, combine, d_logits, key, mixed, token_grad, spread):
    images, patches, slots = dispatch.shape
    widen(spread, arrived, groups)
    for image in range(images):
        returned = pick(spread, 0, image, images, slots)
        mixed[image] = row_dot(combine[image].astype(jnp.bfloat16), returned).astype(jnp.bfloat16)
        d_slot_in = pick(spread, 1, image, images, slots)
        grad = row_dot_t(d_logits[image], key[...])
        grad += row_dot(dispatch[image].astype(jnp.bfloat16), d_slot_in)
        token_grad[image] = grad.astype(jnp.bfloat16)


def finish(arrived, dispatch, combine, d_logits, slot_key_matrix, groups):
    images, patches, slots = dispatch.shape
    width = slot_key_matrix.shape[0]
    shape = jax.ShapeDtypeStruct((images, patches, width), jnp.bfloat16)
    return pl.pallas_call(
        functools.partial(finish_kernel, groups),
        out_shape=(shape, shape),
        in_specs=[pl.BlockSpec(memory_space=pltpu.VMEM)] * 5,
        out_specs=(pl.BlockSpec(memory_space=pltpu.VMEM),) * 2,
        scratch_shapes=[spread_shape(math.prod(arrived.shape[:-1]), arrived.shape[-1])],
        compiler_params=pltpu.CompilerParams(vmem_limit_bytes=VMEM_LIMIT),
        name="finish",
    )(arrived, dispatch, combine, d_logits, slot_key_matrix)


def key_sum_kernel(terms, total):
    part = terms.shape[2]
    own = jnp.zeros(terms.shape[1:], jnp.float32)
    for peer in range(terms.shape[0]):
        own += terms[peer].astype(jnp.float32)
    for half in range(HALVES):
        total[:, half * part : (half + 1) * part] = own[half : half + 1]


def key_sum(terms):
    return pl.pallas_call(
        key_sum_kernel,
        out_shape=jax.ShapeDtypeStruct((1, terms.shape[1] * terms.shape[2]), jnp.float32),
        in_specs=[pl.BlockSpec(memory_space=pltpu.VMEM)],
        out_specs=pl.BlockSpec(memory_space=pltpu.VMEM),
        compiler_params=pltpu.CompilerParams(vmem_limit_bytes=VMEM_LIMIT),
        name="key_sum",
    )(terms)


def exchange(blocks):
    return lax.all_to_all(blocks, EXCHANGE_AXES, split_axis=0, concat_axis=0, tiled=True)


def shards(tokens, slot_key_matrix, w_in, w_out, upstream, groups=4):
    images, patches, width = tokens.shape
    slots = slot_key_matrix.shape[1]
    sent, dispatch, combine, w_out = route(tokens, upstream, slot_key_matrix, w_out, groups)
    by_group = sent.shape
    per_peer, part = by_group[2:]
    arrived = exchange(hold(sent).reshape(slots, per_peer, part))
    answered = expert(arrived.reshape(-1, part), w_in, w_out, images)
    returned = exchange(answered.reshape(slots, per_peer, part)).reshape(by_group)
    d_logits, key_part = logit_grad(returned, tokens, upstream, dispatch, combine, groups)
    key_terms = exchange(key_part.reshape(slots, HALVES, -1))
    mixed, token_grad = finish(returned, dispatch, combine, d_logits, slot_key_matrix, groups)
    key_grad = key_sum(key_terms)
    return (mixed, token_grad, key_grad)


def solution(mesh):
    in_specs = (
        P(AXES, None, None),
        P(),
        P(AXES, None, None),
        P(AXES, None, None),
        P(AXES, None, None),
    )
    out_specs = (P(AXES, None, None), P(AXES, None, None), P(AXES, None))
    body = functools.partial(shards, groups=mesh.shape["group"])
    return jax.shard_map(body, mesh=mesh, in_specs=in_specs, out_specs=out_specs, check_vma=False)
```

```python
import functools
import math

import jax
import jax.numpy as jnp
from jax import lax
from jax.experimental import pallas as pl
from jax.experimental.pallas import tpu as pltpu
from jax.sharding import PartitionSpec as P

AXES = ("group", "member")
EXCHANGE_AXES = ("member", "group")
HALVES = 2
LANES = 128
KINDS = 2
VMEM_LIMIT = 16 * 1024 * 1024
EXPERT_VMEM = 28 * 1024 * 1024
GELU_SCALE = 0.7978845608028654
GELU_CUBIC = 0.044715


def row_dot(a, b):
    return lax.dot_general(a, b, (((1,), (0,)), ((), ())), preferred_element_type=jnp.float32)


def row_dot_t(a, b):
    return lax.dot_general(a, b, (((1,), (1,)), ((), ())), preferred_element_type=jnp.float32)


def col_dot(a, b):
    return lax.dot_general(a, b, (((0,), (0,)), ((), ())), preferred_element_type=jnp.float32)


def place(spread, kind, image, images, rows):
    peers, width = rows.shape
    per_peer = KINDS * images * HALVES
    lane_blocks = spread.shape[0]
    for half in range(HALVES):
        at = (kind * images + image) * HALVES + half
        for block in range(lane_blocks):
            first = (block * HALVES + half) * LANES
            spread[block, pl.ds(at, peers, stride=per_peer), :] = rows[:, first : first + LANES]


def pick(spread, kind, image, images, peers):
    per_peer = KINDS * images * HALVES
    parts = []
    for block in range(spread.shape[0]):
        for half in range(HALVES):
            at = (kind * images + image) * HALVES + half
            rows = spread[block, pl.ds(at, peers, stride=per_peer), :]
            parts.append(rows.astype(jnp.bfloat16))
    return jnp.concatenate(parts, axis=1)


def widen(spread, arrived, groups):
    rows = spread.shape[1] // groups
    for block in range(spread.shape[0]):
        lanes = slice(block * LANES, (block + 1) * LANES)
        for group in range(groups):
            own = arrived[:, group, :, lanes].astype(jnp.float32)
            spread[block, group * rows : (group + 1) * rows, :] = own.reshape(rows, LANES)


def narrow(sent, spread, groups):
    rows = spread.shape[1] // groups
    per_peer = sent.shape[2]
    for block in range(spread.shape[0]):
        lanes = slice(block * LANES, (block + 1) * LANES)
        for group in range(groups):
            own = spread[block, group * rows : (group + 1) * rows, :]
            sent[:, group, :, lanes] = own.reshape(-1, per_peer, LANES).astype(jnp.bfloat16)


def spread_shape(rows, part):
    return pltpu.VMEM((part // LANES, rows, LANES), jnp.float32)


def route_kernel(
    groups,
    tokens_hbm,
    upstream_hbm,
    key_hbm,
    weight_hbm,
    sent,
    dispatch,
    combine,
    weight,
    tokens,
    upstream,
    key,
    spread,
    sems,
):
    images = tokens.shape[0]
    key_copy = pltpu.make_async_copy(key_hbm, key, sems.at[2 * images])
    key_copy.start()
    copies = []
    for place_at, (source, target) in enumerate(((tokens_hbm, tokens), (upstream_hbm, upstream))):
        for image in range(images):
            copy = pltpu.make_async_copy(
                source.at[image], target.at[image], sems.at[2 * image + place_at]
            )
            copy.start()
            copies.append(copy)
    weight_copy = pltpu.make_async_copy(weight_hbm.at[0], weight, sems.at[2 * images + 1])
    weight_copy.start()
    key_copy.wait()
    for image in range(images):
        copies[image].wait()
    slot_weights = []
    patches, width = tokens.shape[1:]
    all_logits = row_dot(tokens[...].reshape(images * patches, width), key[...])
    for image in range(images):
        logits = all_logits[image * patches : (image + 1) * patches]
        by_token = jnp.exp(logits - jnp.max(logits, axis=0, keepdims=True))
        by_token = by_token / jnp.sum(by_token, axis=0, keepdims=True)
        dispatch[image] = by_token
        by_slot = jnp.exp(logits - jnp.max(logits, axis=1, keepdims=True))
        by_slot = by_slot / jnp.sum(by_slot, axis=1, keepdims=True)
        combine[image] = by_slot
        slot_weights.append(by_slot.astype(jnp.bfloat16))
        slot_in = col_dot(by_token.astype(jnp.bfloat16), tokens[image])
        place(spread, 0, image, images, slot_in)
    for image in range(images):
        copies[images + image].wait()
    for image in range(images):
        d_slot_out = col_dot(slot_weights[image], upstream[image])
        place(spread, 1, image, images, d_slot_out)
    narrow(sent, spread, groups)
    weight_copy.wait()


def route(tokens, upstream, slot_key_matrix, weight, groups):
    images, patches, width = tokens.shape
    slots = slot_key_matrix.shape[1]
    per_peer = KINDS * images * HALVES
    rows = slots * per_peer
    part = width // HALVES
    return pl.pallas_call(
        functools.partial(route_kernel, groups),
        out_shape=(
            jax.ShapeDtypeStruct((slots // groups, groups, per_peer, part), jnp.bfloat16),
            jax.ShapeDtypeStruct((images, patches, slots), jnp.float32),
            jax.ShapeDtypeStruct((images, patches, slots), jnp.float32),
            pltpu.VMEM(weight.shape[1:], weight.dtype),
        ),
        in_specs=[pl.BlockSpec(memory_space=pltpu.HBM)] * 4,
        out_specs=(pl.BlockSpec(memory_space=pltpu.VMEM),) * 4,
        scratch_shapes=[
            pltpu.VMEM(tokens.shape, tokens.dtype),
            pltpu.VMEM(upstream.shape, upstream.dtype),
            pltpu.VMEM(slot_key_matrix.shape, slot_key_matrix.dtype),
            spread_shape(rows, part),
            pltpu.SemaphoreType.DMA((2 * images + 2,)),
        ],
        compiler_params=pltpu.CompilerParams(vmem_limit_bytes=VMEM_LIMIT),
        name="route",
    )(*(pltpu.with_memory_space_constraint(x, pltpu.HBM) for x in (tokens, upstream, slot_key_matrix, weight)))


def hold_kernel(rows, out):
    del rows, out


def hold(rows):
    return pl.pallas_call(
        hold_kernel,
        out_shape=jax.ShapeDtypeStruct(rows.shape, rows.dtype),
        in_specs=[pl.BlockSpec(memory_space=pl.ANY)],
        out_specs=pl.BlockSpec(memory_space=pl.ANY),
        input_output_aliases={0: 0},
        cost_estimate=pl.CostEstimate(flops=10**9, bytes_accessed=10**8, transcendentals=10**6),
        compiler_params=pltpu.CompilerParams(vmem_limit_bytes=1024 * 1024),
        name="hold",
    )(rows)


def expert_kernel(images, arrived, w_in, w_out, sent, spread, answers):
    peers = arrived.shape[0] // (KINDS * images * HALVES)
    for block in range(spread.shape[0]):
        lanes = slice(block * LANES, (block + 1) * LANES)
        spread[block] = arrived[:, lanes].astype(jnp.float32)

    def rows_of(kind):
        return jnp.concatenate(
            [pick(spread, kind, image, images, peers) for image in range(images)], axis=0
        )

    def answer(kind, rows, block=None):
        for image in range(images):
            own = rows[image * peers : (image + 1) * peers]
            if block is None:
                place(answers, kind, image, images, own)
            else:
                place(answers.at[pl.ds(block, 1)], kind, image, images, own)

    rows_in, rows_grad = rows_of(0), rows_of(1)
    activated, d_pre = [], []
    units = w_out.shape[0] // 2
    for at in range(2):
        part = slice(at * units, (at + 1) * units)
        d_act = row_dot_t(rows_grad, w_out[part])
        pre = row_dot(rows_in, w_in[0, :, part])
        square = pre * pre
        tanh = jnp.tanh(GELU_SCALE * (pre * (1.0 + GELU_CUBIC * square)))
        gate = 0.5 * (1.0 + tanh)
        slope = gate + 0.5 * pre * (1.0 - tanh * tanh) * (
            GELU_SCALE * (1.0 + 3.0 * GELU_CUBIC * square)
        )
        activated.append((pre * gate).astype(jnp.bfloat16))
        d_pre.append((d_act * slope).astype(jnp.bfloat16))
    activated = jnp.concatenate(activated, axis=1)
    d_pre = jnp.concatenate(d_pre, axis=1)
    answer(0, row_dot(activated, w_out[...]))
    columns = HALVES * LANES
    for block in range(spread.shape[0]):
        rows = slice(block * columns, (block + 1) * columns)
        answer(1, row_dot_t(d_pre, w_in[0, rows]), block)
        lanes = slice(block * LANES, (block + 1) * LANES)
        sent[:, lanes] = answers[block].astype(jnp.bfloat16)


def expert(arrived, w_in, w_out, images):
    def body(*refs):
        expert_kernel(images, *refs)

    return pl.pallas_call(
        body,
        out_shape=jax.ShapeDtypeStruct(arrived.shape, jnp.bfloat16),
        in_specs=[pl.BlockSpec(memory_space=pltpu.VMEM)] * 3,
        out_specs=pl.BlockSpec(memory_space=pltpu.VMEM),
        scratch_shapes=[spread_shape(*arrived.shape), spread_shape(*arrived.shape)],
        compiler_params=pltpu.CompilerParams(vmem_limit_bytes=EXPERT_VMEM),
        name="expert",
    )(arrived, w_in, w_out)


def logit_grad_kernel(
    groups, arrived, tokens, upstream, dispatch, combine, d_logits, key_part, spread
):
    images, patches, width = tokens.shape
    slots = dispatch.shape[2]
    widen(spread, arrived, groups)
    grads = []
    for image in range(images):
        returned = pick(spread, 0, image, images, slots)
        d_slot_in = pick(spread, 1, image, images, slots)
        d_combine = row_dot_t(upstream[image], returned)
        by_slot = combine[image]
        both = by_slot * (d_combine - jnp.sum(by_slot * d_combine, axis=1, keepdims=True))
        d_dispatch = row_dot_t(tokens[image], d_slot_in)
        by_token = dispatch[image]
        both += by_token * (d_dispatch - jnp.sum(by_token * d_dispatch, axis=0, keepdims=True))
        both = both.astype(jnp.bfloat16)
        d_logits[image] = both
        grads.append(both)
    total = col_dot(
        jnp.concatenate(grads, axis=0), tokens[...].reshape(images * patches, width)
    )
    part = width // HALVES
    members = slots // groups
    for half in range(HALVES):
        lanes = total[:, half * part : (half + 1) * part]
        for group in range(groups):
            rows = lanes[group * members : (group + 1) * members]
            key_part[:, group, half, :] = rows.astype(jnp.bfloat16)


def logit_grad(arrived, tokens, upstream, dispatch, combine, groups):
    images, patches, width = tokens.shape
    slots = dispatch.shape[2]
    key_shape = (slots // groups, groups, HALVES, width // HALVES)
    return pl.pallas_call(
        functools.partial(logit_grad_kernel, groups),
        out_shape=(
            jax.ShapeDtypeStruct(dispatch.shape, jnp.bfloat16),
            jax.ShapeDtypeStruct(key_shape, jnp.bfloat16),
        ),
        in_specs=[pl.BlockSpec(memory_space=pltpu.VMEM)] * 5,
        out_specs=(pl.BlockSpec(memory_space=pltpu.VMEM),) * 2,
        scratch_shapes=[spread_shape(math.prod(arrived.shape[:-1]), arrived.shape[-1])],
        compiler_params=pltpu.CompilerParams(vmem_limit_bytes=VMEM_LIMIT),
        name="logit_grad",
    )(arrived, tokens, upstream, dispatch, combine)


def finish_kernel(groups, arrived, dispatch, combine, d_logits, key, mixed, token_grad, spread):
    images, patches, slots = dispatch.shape
    widen(spread, arrived, groups)
    for image in range(images):
        returned = pick(spread, 0, image, images, slots)
        mixed[image] = row_dot(combine[image].astype(jnp.bfloat16), returned).astype(jnp.bfloat16)
        d_slot_in = pick(spread, 1, image, images, slots)
        grad = row_dot_t(d_logits[image], key[...])
        grad += row_dot(dispatch[image].astype(jnp.bfloat16), d_slot_in)
        token_grad[image] = grad.astype(jnp.bfloat16)


def finish(arrived, dispatch, combine, d_logits, slot_key_matrix, groups):
    images, patches, slots = dispatch.shape
    width = slot_key_matrix.shape[0]
    shape = jax.ShapeDtypeStruct((images, patches, width), jnp.bfloat16)
    return pl.pallas_call(
        functools.partial(finish_kernel, groups),
        out_shape=(shape, shape),
        in_specs=[pl.BlockSpec(memory_space=pltpu.VMEM)] * 5,
        out_specs=(pl.BlockSpec(memory_space=pltpu.VMEM),) * 2,
        scratch_shapes=[spread_shape(math.prod(arrived.shape[:-1]), arrived.shape[-1])],
        compiler_params=pltpu.CompilerParams(vmem_limit_bytes=VMEM_LIMIT),
        name="finish",
    )(arrived, dispatch, combine, d_logits, slot_key_matrix)


def key_sum_kernel(terms, total):
    part = terms.shape[2]
    own = jnp.zeros(terms.shape[1:], jnp.float32)
    for peer in range(terms.shape[0]):
        own += terms[peer].astype(jnp.float32)
    for half in range(HALVES):
        total[:, half * part : (half + 1) * part] = own[half : half + 1]


def key_sum(terms):
    return pl.pallas_call(
        key_sum_kernel,
        out_shape=jax.ShapeDtypeStruct((1, terms.shape[1] * terms.shape[2]), jnp.float32),
        in_specs=[pl.BlockSpec(memory_space=pltpu.VMEM)],
        out_specs=pl.BlockSpec(memory_space=pltpu.VMEM),
        compiler_params=pltpu.CompilerParams(vmem_limit_bytes=VMEM_LIMIT),
        name="key_sum",
    )(terms)


def exchange(blocks):
    return lax.all_to_all(blocks, EXCHANGE_AXES, split_axis=0, concat_axis=0, tiled=True)


def shards(tokens, slot_key_matrix, w_in, w_out, upstream, groups=4):
    images, patches, width = tokens.shape
    slots = slot_key_matrix.shape[1]
    sent, dispatch, combine, w_out = route(tokens, upstream, slot_key_matrix, w_out, groups)
    by_group = sent.shape
    per_peer, part = by_group[2:]
    arrived = exchange(hold(sent).reshape(slots, per_peer, part))
    answered = expert(arrived.reshape(-1, part), w_in, w_out, images)
    returned = exchange(answered.reshape(slots, per_peer, part)).reshape(by_group)
    d_logits, key_part = logit_grad(returned, tokens, upstream, dispatch, combine, groups)
    key_terms = exchange(key_part.reshape(slots, HALVES, -1))
    mixed, token_grad = finish(returned, dispatch, combine, d_logits, slot_key_matrix, groups)
    key_grad = key_sum(key_terms)
    return (mixed, token_grad, key_grad)


def solution(mesh):
    in_specs = (
        P(AXES, None, None),
        P(),
        P(AXES, None, None),
        P(AXES, None, None),
        P(AXES, None, None),
    )
    out_specs = (P(AXES, None, None), P(AXES, None, None), P(AXES, None))
    body = functools.partial(shards, groups=mesh.shape["group"])
    return jax.shard_map(body, mesh=mesh, in_specs=in_specs, out_specs=out_specs, check_vma=False)
```

```python
import functools
import math

import jax
import jax.numpy as jnp
from jax import lax
from jax.experimental import pallas as pl
from jax.experimental.pallas import tpu as pltpu
from jax.sharding import PartitionSpec as P

AXES = ("group", "member")
EXCHANGE_AXES = ("member", "group")
HALVES = 2
LANES = 128
KINDS = 2
VMEM_LIMIT = 16 * 1024 * 1024
EXPERT_VMEM = 28 * 1024 * 1024
GELU_SCALE = 0.7978845608028654
GELU_CUBIC = 0.044715


def row_dot(a, b):
    return lax.dot_general(a, b, (((1,), (0,)), ((), ())), preferred_element_type=jnp.float32)


def row_dot_t(a, b):
    return lax.dot_general(a, b, (((1,), (1,)), ((), ())), preferred_element_type=jnp.float32)


def col_dot(a, b):
    return lax.dot_general(a, b, (((0,), (0,)), ((), ())), preferred_element_type=jnp.float32)


def place(spread, kind, image, images, rows):
    peers, width = rows.shape
    per_peer = KINDS * images * HALVES
    lane_blocks = spread.shape[0]
    for half in range(HALVES):
        at = (kind * images + image) * HALVES + half
        for block in range(lane_blocks):
            first = (block * HALVES + half) * LANES
            spread[block, pl.ds(at, peers, stride=per_peer), :] = rows[:, first : first + LANES]


def pick(spread, kind, image, images, peers):
    per_peer = KINDS * images * HALVES
    parts = []
    for block in range(spread.shape[0]):
        for half in range(HALVES):
            at = (kind * images + image) * HALVES + half
            rows = spread[block, pl.ds(at, peers, stride=per_peer), :]
            parts.append(rows.astype(jnp.bfloat16))
    return jnp.concatenate(parts, axis=1)


def widen(spread, arrived, groups):
    rows = spread.shape[1] // groups
    for block in range(spread.shape[0]):
        lanes = slice(block * LANES, (block + 1) * LANES)
        for group in range(groups):
            own = arrived[:, group, :, lanes].astype(jnp.float32)
            spread[block, group * rows : (group + 1) * rows, :] = own.reshape(rows, LANES)


def narrow(sent, spread, groups):
    rows = spread.shape[1] // groups
    per_peer = sent.shape[2]
    for block in range(spread.shape[0]):
        lanes = slice(block * LANES, (block + 1) * LANES)
        for group in range(groups):
            own = spread[block, group * rows : (group + 1) * rows, :]
            sent[:, group, :, lanes] = own.reshape(-1, per_peer, LANES).astype(jnp.bfloat16)


def spread_shape(rows, part):
    return pltpu.VMEM((part // LANES, rows, LANES), jnp.float32)


def route_kernel(
    groups,
    tokens_hbm,
    upstream_hbm,
    key_hbm,
    weight_hbm,
    sent,
    dispatch,
    combine,
    weight,
    tokens,
    upstream,
    key,
    spread,
    sems,
):
    images = tokens.shape[0]
    key_copy = pltpu.make_async_copy(key_hbm, key, sems.at[2 * images])
    key_copy.start()
    copies = []
    for place_at, (source, target) in enumerate(((tokens_hbm, tokens), (upstream_hbm, upstream))):
        for image in range(images):
            copy = pltpu.make_async_copy(
                source.at[image], target.at[image], sems.at[2 * image + place_at]
            )
            copy.start()
            copies.append(copy)
    weight_copy = pltpu.make_async_copy(weight_hbm.at[0], weight, sems.at[2 * images + 1])
    weight_copy.start()
    key_copy.wait()
    for image in range(images):
        copies[image].wait()
    slot_weights = []
    patches, width = tokens.shape[1:]
    all_logits = row_dot(tokens[...].reshape(images * patches, width), key[...])
    for image in range(images):
        logits = all_logits[image * patches : (image + 1) * patches]
        by_token = jnp.exp(logits - jnp.max(logits, axis=0, keepdims=True))
        by_token = by_token * (1.0 / jnp.sum(by_token, axis=0, keepdims=True))
        dispatch[image] = by_token
        by_slot = jnp.exp(logits - jnp.max(logits, axis=1, keepdims=True))
        by_slot = by_slot * (1.0 / jnp.sum(by_slot, axis=1, keepdims=True))
        combine[image] = by_slot
        slot_weights.append(by_slot.astype(jnp.bfloat16))
        slot_in = col_dot(by_token.astype(jnp.bfloat16), tokens[image])
        place(spread, 0, image, images, slot_in)
    for image in range(images):
        copies[images + image].wait()
    for image in range(images):
        d_slot_out = col_dot(slot_weights[image], upstream[image])
        place(spread, 1, image, images, d_slot_out)
    narrow(sent, spread, groups)
    weight_copy.wait()


def route(tokens, upstream, slot_key_matrix, weight, groups):
    images, patches, width = tokens.shape
    slots = slot_key_matrix.shape[1]
    per_peer = KINDS * images * HALVES
    rows = slots * per_peer
    part = width // HALVES
    return pl.pallas_call(
        functools.partial(route_kernel, groups),
        out_shape=(
            jax.ShapeDtypeStruct((slots // groups, groups, per_peer, part), jnp.bfloat16),
            jax.ShapeDtypeStruct((images, patches, slots), jnp.float32),
            jax.ShapeDtypeStruct((images, patches, slots), jnp.float32),
            pltpu.VMEM(weight.shape[1:], weight.dtype),
        ),
        in_specs=[pl.BlockSpec(memory_space=pltpu.HBM)] * 4,
        out_specs=(pl.BlockSpec(memory_space=pltpu.VMEM),) * 4,
        scratch_shapes=[
            pltpu.VMEM(tokens.shape, tokens.dtype),
            pltpu.VMEM(upstream.shape, upstream.dtype),
            pltpu.VMEM(slot_key_matrix.shape, slot_key_matrix.dtype),
            spread_shape(rows, part),
            pltpu.SemaphoreType.DMA((2 * images + 2,)),
        ],
        compiler_params=pltpu.CompilerParams(vmem_limit_bytes=VMEM_LIMIT),
        name="route",
    )(*(pltpu.with_memory_space_constraint(x, pltpu.HBM) for x in (tokens, upstream, slot_key_matrix, weight)))


def hold_kernel(rows, out):
    del rows, out


def hold(rows):
    return pl.pallas_call(
        hold_kernel,
        out_shape=jax.ShapeDtypeStruct(rows.shape, rows.dtype),
        in_specs=[pl.BlockSpec(memory_space=pl.ANY)],
        out_specs=pl.BlockSpec(memory_space=pl.ANY),
        input_output_aliases={0: 0},
        cost_estimate=pl.CostEstimate(flops=10**9, bytes_accessed=10**8, transcendentals=10**6),
        compiler_params=pltpu.CompilerParams(vmem_limit_bytes=1024 * 1024),
        name="hold",
    )(rows)


def expert_kernel(images, arrived, w_in, w_out, sent, spread, answers):
    peers = arrived.shape[0] // (KINDS * images * HALVES)
    for block in range(spread.shape[0]):
        lanes = slice(block * LANES, (block + 1) * LANES)
        spread[block] = arrived[:, lanes].astype(jnp.float32)

    def rows_of(kind):
        return jnp.concatenate(
            [pick(spread, kind, image, images, peers) for image in range(images)], axis=0
        )

    def answer(kind, rows, block=None):
        for image in range(images):
            own = rows[image * peers : (image + 1) * peers]
            if block is None:
                place(answers, kind, image, images, own)
            else:
                place(answers.at[pl.ds(block, 1)], kind, image, images, own)

    rows_in, rows_grad = rows_of(0), rows_of(1)
    activated, d_pre = [], []
    units = w_out.shape[0] // 2
    for at in range(2):
        part = slice(at * units, (at + 1) * units)
        d_act = row_dot_t(rows_grad, w_out[part])
        pre = row_dot(rows_in, w_in[0, :, part])
        square = pre * pre
        tanh = jnp.tanh(GELU_SCALE * (pre * (1.0 + GELU_CUBIC * square)))
        gate = 0.5 * (1.0 + tanh)
        slope = gate + 0.5 * pre * (1.0 - tanh * tanh) * (
            GELU_SCALE * (1.0 + 3.0 * GELU_CUBIC * square)
        )
        activated.append((pre * gate).astype(jnp.bfloat16))
        d_pre.append((d_act * slope).astype(jnp.bfloat16))
    activated = jnp.concatenate(activated, axis=1)
    d_pre = jnp.concatenate(d_pre, axis=1)
    answer(0, row_dot(activated, w_out[...]))
    columns = HALVES * LANES
    for block in range(spread.shape[0]):
        rows = slice(block * columns, (block + 1) * columns)
        answer(1, row_dot_t(d_pre, w_in[0, rows]), block)
        lanes = slice(block * LANES, (block + 1) * LANES)
        sent[:, lanes] = answers[block].astype(jnp.bfloat16)


def expert(arrived, w_in, w_out, images):
    def body(*refs):
        expert_kernel(images, *refs)

    return pl.pallas_call(
        body,
        out_shape=jax.ShapeDtypeStruct(arrived.shape, jnp.bfloat16),
        in_specs=[pl.BlockSpec(memory_space=pltpu.VMEM)] * 3,
        out_specs=pl.BlockSpec(memory_space=pltpu.VMEM),
        scratch_shapes=[spread_shape(*arrived.shape), spread_shape(*arrived.shape)],
        compiler_params=pltpu.CompilerParams(vmem_limit_bytes=EXPERT_VMEM),
        name="expert",
    )(arrived, w_in, w_out)


def logit_grad_kernel(
    groups, arrived, tokens, upstream, dispatch, combine, d_logits, key_part, spread
):
    images, patches, width = tokens.shape
    slots = dispatch.shape[2]
    widen(spread, arrived, groups)
    grads = []
    for image in range(images):
        returned = pick(spread, 0, image, images, slots)
        d_slot_in = pick(spread, 1, image, images, slots)
        d_combine = row_dot_t(upstream[image], returned)
        by_slot = combine[image]
        both = by_slot * (d_combine - jnp.sum(by_slot * d_combine, axis=1, keepdims=True))
        d_dispatch = row_dot_t(tokens[image], d_slot_in)
        by_token = dispatch[image]
        both += by_token * (d_dispatch - jnp.sum(by_token * d_dispatch, axis=0, keepdims=True))
        both = both.astype(jnp.bfloat16)
        d_logits[image] = both
        grads.append(both)
    total = col_dot(
        jnp.concatenate(grads, axis=0), tokens[...].reshape(images * patches, width)
    )
    part = width // HALVES
    members = slots // groups
    for half in range(HALVES):
        lanes = total[:, half * part : (half + 1) * part]
        for group in range(groups):
            rows = lanes[group * members : (group + 1) * members]
            key_part[:, group, half, :] = rows.astype(jnp.bfloat16)


def logit_grad(arrived, tokens, upstream, dispatch, combine, groups):
    images, patches, width = tokens.shape
    slots = dispatch.shape[2]
    key_shape = (slots // groups, groups, HALVES, width // HALVES)
    return pl.pallas_call(
        functools.partial(logit_grad_kernel, groups),
        out_shape=(
            jax.ShapeDtypeStruct(dispatch.shape, jnp.bfloat16),
            jax.ShapeDtypeStruct(key_shape, jnp.bfloat16),
        ),
        in_specs=[pl.BlockSpec(memory_space=pltpu.VMEM)] * 5,
        out_specs=(pl.BlockSpec(memory_space=pltpu.VMEM),) * 2,
        scratch_shapes=[spread_shape(math.prod(arrived.shape[:-1]), arrived.shape[-1])],
        compiler_params=pltpu.CompilerParams(vmem_limit_bytes=VMEM_LIMIT),
        name="logit_grad",
    )(arrived, tokens, upstream, dispatch, combine)


def finish_kernel(groups, arrived, dispatch, combine, d_logits, key, mixed, token_grad, spread):
    images, patches, slots = dispatch.shape
    widen(spread, arrived, groups)
    for image in range(images):
        returned = pick(spread, 0, image, images, slots)
        mixed[image] = row_dot(combine[image].astype(jnp.bfloat16), returned).astype(jnp.bfloat16)
        d_slot_in = pick(spread, 1, image, images, slots)
        grad = row_dot_t(d_logits[image], key[...])
        grad += row_dot(dispatch[image].astype(jnp.bfloat16), d_slot_in)
        token_grad[image] = grad.astype(jnp.bfloat16)


def finish(arrived, dispatch, combine, d_logits, slot_key_matrix, groups):
    images, patches, slots = dispatch.shape
    width = slot_key_matrix.shape[0]
    shape = jax.ShapeDtypeStruct((images, patches, width), jnp.bfloat16)
    return pl.pallas_call(
        functools.partial(finish_kernel, groups),
        out_shape=(shape, shape),
        in_specs=[pl.BlockSpec(memory_space=pltpu.VMEM)] * 5,
        out_specs=(pl.BlockSpec(memory_space=pltpu.VMEM),) * 2,
        scratch_shapes=[spread_shape(math.prod(arrived.shape[:-1]), arrived.shape[-1])],
        compiler_params=pltpu.CompilerParams(vmem_limit_bytes=VMEM_LIMIT),
        name="finish",
    )(arrived, dispatch, combine, d_logits, slot_key_matrix)


def key_sum_kernel(terms, total):
    part = terms.shape[2]
    own = jnp.zeros(terms.shape[1:], jnp.float32)
    for peer in range(terms.shape[0]):
        own += terms[peer].astype(jnp.float32)
    for half in range(HALVES):
        total[:, half * part : (half + 1) * part] = own[half : half + 1]


def key_sum(terms):
    return pl.pallas_call(
        key_sum_kernel,
        out_shape=jax.ShapeDtypeStruct((1, terms.shape[1] * terms.shape[2]), jnp.float32),
        in_specs=[pl.BlockSpec(memory_space=pltpu.VMEM)],
        out_specs=pl.BlockSpec(memory_space=pltpu.VMEM),
        compiler_params=pltpu.CompilerParams(vmem_limit_bytes=VMEM_LIMIT),
        name="key_sum",
    )(terms)


def exchange(blocks):
    return lax.all_to_all(blocks, EXCHANGE_AXES, split_axis=0, concat_axis=0, tiled=True)


def shards(tokens, slot_key_matrix, w_in, w_out, upstream, groups=4):
    images, patches, width = tokens.shape
    slots = slot_key_matrix.shape[1]
    sent, dispatch, combine, w_out = route(tokens, upstream, slot_key_matrix, w_out, groups)
    by_group = sent.shape
    per_peer, part = by_group[2:]
    arrived = exchange(hold(sent).reshape(slots, per_peer, part))
    answered = expert(arrived.reshape(-1, part), w_in, w_out, images)
    returned = exchange(answered.reshape(slots, per_peer, part)).reshape(by_group)
    d_logits, key_part = logit_grad(returned, tokens, upstream, dispatch, combine, groups)
    key_terms = exchange(key_part.reshape(slots, HALVES, -1))
    mixed, token_grad = finish(returned, dispatch, combine, d_logits, slot_key_matrix, groups)
    key_grad = key_sum(key_terms)
    return (mixed, token_grad, key_grad)


def solution(mesh):
    in_specs = (
        P(AXES, None, None),
        P(),
        P(AXES, None, None),
        P(AXES, None, None),
        P(AXES, None, None),
    )
    out_specs = (P(AXES, None, None), P(AXES, None, None), P(AXES, None))
    body = functools.partial(shards, groups=mesh.shape["group"])
    return jax.shard_map(body, mesh=mesh, in_specs=in_specs, out_specs=out_specs, check_vma=False)
```

```python
import functools
import math

import jax
import jax.numpy as jnp
from jax import lax
from jax.experimental import pallas as pl
from jax.experimental.pallas import tpu as pltpu
from jax.sharding import PartitionSpec as P

AXES = ("group", "member")
EXCHANGE_AXES = ("member", "group")
HALVES = 2
LANES = 128
KINDS = 2
VMEM_LIMIT = 16 * 1024 * 1024
EXPERT_VMEM = 28 * 1024 * 1024
GELU_SCALE = 0.7978845608028654
GELU_CUBIC = 0.044715


def row_dot(a, b):
    return lax.dot_general(a, b, (((1,), (0,)), ((), ())), preferred_element_type=jnp.float32)


def row_dot_t(a, b):
    return lax.dot_general(a, b, (((1,), (1,)), ((), ())), preferred_element_type=jnp.float32)


def col_dot(a, b):
    return lax.dot_general(a, b, (((0,), (0,)), ((), ())), preferred_element_type=jnp.float32)


def place(spread, kind, image, images, rows):
    peers, width = rows.shape
    per_peer = KINDS * images * HALVES
    lane_blocks = spread.shape[0]
    for half in range(HALVES):
        at = (kind * images + image) * HALVES + half
        for block in range(lane_blocks):
            first = (block * HALVES + half) * LANES
            spread[block, pl.ds(at, peers, stride=per_peer), :] = rows[:, first : first + LANES]


def pick(spread, kind, image, images, peers):
    per_peer = KINDS * images * HALVES
    parts = []
    for block in range(spread.shape[0]):
        for half in range(HALVES):
            at = (kind * images + image) * HALVES + half
            rows = spread[block, pl.ds(at, peers, stride=per_peer), :]
            parts.append(rows.astype(jnp.bfloat16))
    return jnp.concatenate(parts, axis=1)


def widen(spread, arrived, groups):
    rows = spread.shape[1] // groups
    for block in range(spread.shape[0]):
        lanes = slice(block * LANES, (block + 1) * LANES)
        for group in range(groups):
            own = arrived[:, group, :, lanes].astype(jnp.float32)
            spread[block, group * rows : (group + 1) * rows, :] = own.reshape(rows, LANES)


def narrow(sent, spread, groups):
    rows = spread.shape[1] // groups
    per_peer = sent.shape[2]
    for block in range(spread.shape[0]):
        lanes = slice(block * LANES, (block + 1) * LANES)
        for group in range(groups):
            own = spread[block, group * rows : (group + 1) * rows, :]
            sent[:, group, :, lanes] = own.reshape(-1, per_peer, LANES).astype(jnp.bfloat16)


def spread_shape(rows, part):
    return pltpu.VMEM((part // LANES, rows, LANES), jnp.float32)


def route_kernel(
    groups,
    tokens_hbm,
    upstream_hbm,
    key_hbm,
    weight_hbm,
    sent,
    dispatch,
    combine,
    weight,
    tokens,
    upstream,
    key,
    spread,
    sems,
):
    images = tokens.shape[0]
    key_copy = pltpu.make_async_copy(key_hbm, key, sems.at[2 * images])
    key_copy.start()
    copies = []
    for place_at, (source, target) in enumerate(((tokens_hbm, tokens), (upstream_hbm, upstream))):
        for image in range(images):
            copy = pltpu.make_async_copy(
                source.at[image], target.at[image], sems.at[2 * image + place_at]
            )
            copy.start()
            copies.append(copy)
    weight_copy = pltpu.make_async_copy(weight_hbm.at[0], weight, sems.at[2 * images + 1])
    weight_copy.start()
    key_copy.wait()
    for image in range(images):
        copies[image].wait()
    slot_weights = []
    patches, width = tokens.shape[1:]
    all_logits = row_dot(tokens[...].reshape(images * patches, width), key[...])
    for image in range(images):
        logits = all_logits[image * patches : (image + 1) * patches]
        by_token = jnp.exp(logits - jnp.max(logits, axis=0, keepdims=True))
        by_token = by_token * (1.0 / jnp.sum(by_token, axis=0, keepdims=True))
        dispatch[image] = by_token
        by_slot = jnp.exp(logits - jnp.max(logits, axis=1, keepdims=True))
        by_slot = by_slot * (1.0 / jnp.sum(by_slot, axis=1, keepdims=True))
        combine[image] = by_slot
        slot_weights.append(by_slot.astype(jnp.bfloat16))
        slot_in = col_dot(by_token.astype(jnp.bfloat16), tokens[image])
        place(spread, 0, image, images, slot_in)
    for image in range(images):
        copies[images + image].wait()
    for image in range(images):
        d_slot_out = col_dot(slot_weights[image], upstream[image])
        place(spread, 1, image, images, d_slot_out)
    narrow(sent, spread, groups)
    weight_copy.wait()


def route(tokens, upstream, slot_key_matrix, weight, groups):
    images, patches, width = tokens.shape
    slots = slot_key_matrix.shape[1]
    per_peer = KINDS * images * HALVES
    rows = slots * per_peer
    part = width // HALVES
    return pl.pallas_call(
        functools.partial(route_kernel, groups),
        out_shape=(
            jax.ShapeDtypeStruct((slots // groups, groups, per_peer, part), jnp.bfloat16),
            jax.ShapeDtypeStruct((images, patches, slots), jnp.float32),
            jax.ShapeDtypeStruct((images, patches, slots), jnp.float32),
            pltpu.VMEM(weight.shape[1:], weight.dtype),
        ),
        in_specs=[pl.BlockSpec(memory_space=pltpu.HBM)] * 4,
        out_specs=(pl.BlockSpec(memory_space=pltpu.VMEM),) * 4,
        scratch_shapes=[
            pltpu.VMEM(tokens.shape, tokens.dtype),
            pltpu.VMEM(upstream.shape, upstream.dtype),
            pltpu.VMEM(slot_key_matrix.shape, slot_key_matrix.dtype),
            spread_shape(rows, part),
            pltpu.SemaphoreType.DMA((2 * images + 2,)),
        ],
        compiler_params=pltpu.CompilerParams(vmem_limit_bytes=VMEM_LIMIT),
        name="route",
    )(*(pltpu.with_memory_space_constraint(x, pltpu.HBM) for x in (tokens, upstream, slot_key_matrix, weight)))


def hold_kernel(rows, out):
    del rows, out


def hold(rows):
    return pl.pallas_call(
        hold_kernel,
        out_shape=jax.ShapeDtypeStruct(rows.shape, rows.dtype),
        in_specs=[pl.BlockSpec(memory_space=pl.ANY)],
        out_specs=pl.BlockSpec(memory_space=pl.ANY),
        input_output_aliases={0: 0},
        cost_estimate=pl.CostEstimate(flops=10**9, bytes_accessed=10**8, transcendentals=10**6),
        compiler_params=pltpu.CompilerParams(vmem_limit_bytes=1024 * 1024),
        name="hold",
    )(rows)


def expert_kernel(images, arrived, w_in, w_out, sent, spread, answers):
    peers = arrived.shape[0] // (KINDS * images * HALVES)
    for block in range(spread.shape[0]):
        lanes = slice(block * LANES, (block + 1) * LANES)
        spread[block] = arrived[:, lanes].astype(jnp.float32)

    def rows_of(kind):
        return jnp.concatenate(
            [pick(spread, kind, image, images, peers) for image in range(images)], axis=0
        )

    def answer(kind, rows, block=None):
        for image in range(images):
            own = rows[image * peers : (image + 1) * peers]
            if block is None:
                place(answers, kind, image, images, own)
            else:
                place(answers.at[pl.ds(block, 1)], kind, image, images, own)

    rows_in, rows_grad = rows_of(0), rows_of(1)
    activated, d_pre = [], []
    units = w_out.shape[0] // 2
    for at in range(2):
        part = slice(at * units, (at + 1) * units)
        d_act = row_dot_t(rows_grad, w_out[part])
        pre = row_dot(rows_in, w_in[0, :, part])
        square = pre * pre
        tanh = jnp.tanh(GELU_SCALE * (pre * (1.0 + GELU_CUBIC * square)))
        gate = 0.5 * (1.0 + tanh)
        slope = gate + 0.5 * pre * (1.0 - tanh * tanh) * (
            GELU_SCALE * (1.0 + 3.0 * GELU_CUBIC * square)
        )
        activated.append((pre * gate).astype(jnp.bfloat16))
        d_pre.append((d_act * slope).astype(jnp.bfloat16))
    activated = jnp.concatenate(activated, axis=1)
    d_pre = jnp.concatenate(d_pre, axis=1)
    answer(0, row_dot(activated, w_out[...]))
    columns = HALVES * LANES
    for block in range(spread.shape[0]):
        rows = slice(block * columns, (block + 1) * columns)
        answer(1, row_dot_t(d_pre, w_in[0, rows]), block)
        lanes = slice(block * LANES, (block + 1) * LANES)
        sent[:, lanes] = answers[block].astype(jnp.bfloat16)


def expert(arrived, w_in, w_out, images):
    def body(*refs):
        expert_kernel(images, *refs)

    return pl.pallas_call(
        body,
        out_shape=jax.ShapeDtypeStruct(arrived.shape, jnp.bfloat16),
        in_specs=[pl.BlockSpec(memory_space=pltpu.VMEM)] * 3,
        out_specs=pl.BlockSpec(memory_space=pltpu.VMEM),
        scratch_shapes=[spread_shape(*arrived.shape), spread_shape(*arrived.shape)],
        compiler_params=pltpu.CompilerParams(vmem_limit_bytes=EXPERT_VMEM),
        name="expert",
    )(arrived, w_in, w_out)


def logit_grad_kernel(
    groups, arrived, tokens, upstream, dispatch, combine, d_logits, key_part, spread
):
    images, patches, width = tokens.shape
    slots = dispatch.shape[2]
    widen(spread, arrived, groups)
    grads = []
    for image in range(images):
        returned = pick(spread, 0, image, images, slots)
        d_slot_in = pick(spread, 1, image, images, slots)
        d_combine = row_dot_t(upstream[image], returned)
        by_slot = combine[image]
        both = by_slot * (d_combine - jnp.sum(by_slot * d_combine, axis=1, keepdims=True))
        d_dispatch = row_dot_t(tokens[image], d_slot_in)
        by_token = dispatch[image]
        both += by_token * (d_dispatch - jnp.sum(by_token * d_dispatch, axis=0, keepdims=True))
        both = both.astype(jnp.bfloat16)
        d_logits[image] = both
        grads.append(both)
    total = col_dot(
        jnp.concatenate(grads, axis=0), tokens[...].reshape(images * patches, width)
    )
    part = width // HALVES
    members = slots // groups
    for half in range(HALVES):
        lanes = total[:, half * part : (half + 1) * part]
        for group in range(groups):
            rows = lanes[group * members : (group + 1) * members]
            key_part[:, group, half, :] = rows.astype(jnp.bfloat16)


def logit_grad(arrived, tokens, upstream, dispatch, combine, groups):
    images, patches, width = tokens.shape
    slots = dispatch.shape[2]
    key_shape = (slots // groups, groups, HALVES, width // HALVES)
    return pl.pallas_call(
        functools.partial(logit_grad_kernel, groups),
        out_shape=(
            jax.ShapeDtypeStruct(dispatch.shape, jnp.bfloat16),
            jax.ShapeDtypeStruct(key_shape, jnp.bfloat16),
        ),
        in_specs=[pl.BlockSpec(memory_space=pltpu.VMEM)] * 5,
        out_specs=(pl.BlockSpec(memory_space=pltpu.VMEM),) * 2,
        scratch_shapes=[spread_shape(math.prod(arrived.shape[:-1]), arrived.shape[-1])],
        compiler_params=pltpu.CompilerParams(vmem_limit_bytes=VMEM_LIMIT),
        name="logit_grad",
    )(arrived, tokens, upstream, dispatch, combine)


def finish_kernel(groups, arrived, dispatch, combine, d_logits, key, mixed, token_grad, spread):
    images, patches, slots = dispatch.shape
    widen(spread, arrived, groups)
    for image in range(images):
        returned = pick(spread, 0, image, images, slots)
        mixed[image] = row_dot(combine[image].astype(jnp.bfloat16), returned).astype(jnp.bfloat16)
        d_slot_in = pick(spread, 1, image, images, slots)
        grad = row_dot_t(d_logits[image], key[...])
        grad += row_dot(dispatch[image].astype(jnp.bfloat16), d_slot_in)
        token_grad[image] = grad.astype(jnp.bfloat16)


def finish(arrived, dispatch, combine, d_logits, slot_key_matrix, groups):
    images, patches, slots = dispatch.shape
    width = slot_key_matrix.shape[0]
    shape = jax.ShapeDtypeStruct((images, patches, width), jnp.bfloat16)
    return pl.pallas_call(
        functools.partial(finish_kernel, groups),
        out_shape=(shape, shape),
        in_specs=[pl.BlockSpec(memory_space=pltpu.VMEM)] * 5,
        out_specs=(pl.BlockSpec(memory_space=pltpu.VMEM),) * 2,
        scratch_shapes=[spread_shape(math.prod(arrived.shape[:-1]), arrived.shape[-1])],
        compiler_params=pltpu.CompilerParams(vmem_limit_bytes=VMEM_LIMIT),
        name="finish",
    )(arrived, dispatch, combine, d_logits, slot_key_matrix)


def key_sum_kernel(terms, total):
    part = terms.shape[2]
    half_way = terms.shape[0] // 2
    own = terms[0].astype(jnp.float32)
    rest = terms[half_way].astype(jnp.float32)
    for peer in range(1, half_way):
        own += terms[peer].astype(jnp.float32)
        rest += terms[half_way + peer].astype(jnp.float32)
    own += rest
    for half in range(HALVES):
        total[:, half * part : (half + 1) * part] = own[half : half + 1]


def key_sum(terms):
    return pl.pallas_call(
        key_sum_kernel,
        out_shape=jax.ShapeDtypeStruct((1, terms.shape[1] * terms.shape[2]), jnp.float32),
        in_specs=[pl.BlockSpec(memory_space=pltpu.VMEM)],
        out_specs=pl.BlockSpec(memory_space=pltpu.VMEM),
        compiler_params=pltpu.CompilerParams(vmem_limit_bytes=VMEM_LIMIT),
        name="key_sum",
    )(terms)


def exchange(blocks):
    return lax.all_to_all(blocks, EXCHANGE_AXES, split_axis=0, concat_axis=0, tiled=True)


def shards(tokens, slot_key_matrix, w_in, w_out, upstream, groups=4):
    images, patches, width = tokens.shape
    slots = slot_key_matrix.shape[1]
    sent, dispatch, combine, w_out = route(tokens, upstream, slot_key_matrix, w_out, groups)
    by_group = sent.shape
    per_peer, part = by_group[2:]
    arrived = exchange(hold(sent).reshape(slots, per_peer, part))
    answered = expert(arrived.reshape(-1, part), w_in, w_out, images)
    returned = exchange(answered.reshape(slots, per_peer, part)).reshape(by_group)
    d_logits, key_part = logit_grad(returned, tokens, upstream, dispatch, combine, groups)
    key_terms = exchange(key_part.reshape(slots, HALVES, -1))
    mixed, token_grad = finish(returned, dispatch, combine, d_logits, slot_key_matrix, groups)
    key_grad = key_sum(key_terms)
    return (mixed, token_grad, key_grad)


def solution(mesh):
    in_specs = (
        P(AXES, None, None),
        P(),
        P(AXES, None, None),
        P(AXES, None, None),
        P(AXES, None, None),
    )
    out_specs = (P(AXES, None, None), P(AXES, None, None), P(AXES, None))
    body = functools.partial(shards, groups=mesh.shape["group"])
    return jax.shard_map(body, mesh=mesh, in_specs=in_specs, out_specs=out_specs, check_vma=False)
```
